256 devices in a mesh: clip: 16 (over x, y), tm: 16 (over z, core).
Axes of the slice: x: 4, y: 4, z: 8, core: 2. Of those that a mesh axis runs over, the one named last changes fastest.
Arguments:
- x_inner: bfloat16 [256, 192, 2048], P(('clip', 'tm')), parts along dimension 0, may hold values from -6 to 6
- bc_inputs: bfloat16 [256, 192, 256], P(('clip', 'tm')), parts along dimension 0, may hold values from -2 to 2
- step_raw: bfloat16 [256, 192, 64], P(('clip', 'tm')), parts along dimension 0, may hold values from -5 to 5
- decay_rate: float32 [2, 32], replicated, may hold values from 0.002 to 0.3
- skip_gain: float32 [32], replicated, may hold values from 0.1 to 1.9
- w_out: bfloat16 [2048, 1024], P('tm'), may hold values from -0.125 to 0.125
- grad_out: bfloat16 [256, 192, 1024], P(('clip', 'tm')), parts along dimension 0, may hold values from -6 to 6
Outputs:
- mixed_out: bfloat16 [256, 192, 1024], P(('clip', 'tm')), parts along dimension 0
- grad_inner: bfloat16 [256, 192, 2048], P(('clip', 'tm')), parts along dimension 0
- grad_bc: bfloat16 [256, 192, 256], P(('clip', 'tm')), parts along dimension 0
- grad_step: bfloat16 [256, 192, 64], P(('clip', 'tm')), parts along dimension 0
- grad_w_out: float32 [32768, 1024], P(('clip', 'tm')), parts along dimension 0
The draws below stay inside these ranges and needn't reach their ends.
There are 16 independent parts, one for each index of `clip`. The reference program is written for one: setup_inputs(seed, part) draws one part's arguments, and reference() takes and returns one part's arrays. A program takes and returns all parts, laid end to end along the dimension named above; an argument that names none is the same for every part. Nothing has to cross between parts.
All inputs are finite; a program needn't handle non-finite values.
Results may differ from the reference program's by a relative error of at most 0.022.
Values may be sent and summed in bfloat16 or wider, within the bound.
No kernel may reach another device: no remote copies, remote signals or barrier semaphores. Data moves between devices by JAX's collectives and lax.ppermute only.
A program may use at most 128 MiB of HBM per device.

```python
import math
import jax
import jax.numpy as jnp
from jax import lax

D = 1024
H = 32
N = 64
P_SIZE = 192
E = 2048
FRAMES = 16


def levels(stream_key, dims, cuts, smallest, top_value):
    def one(position, shards_of):
        steps = jax.random.uniform(jax.random.fold_in(jax.random.fold_in(stream_key, 6), position), (shards_of,), jnp.float32, smallest / len(cuts), top_value / len(cuts))
        return jnp.repeat(jnp.exp(steps), dims[position] // shards_of).reshape((-1,) + (1,) * (len(dims) - position - 1))

    factor_of = one(*cuts[0])
    for cut in cuts[1:]:
        factor_of = factor_of * one(*cut)
    return factor_of


def gaussian(rng, extent, width, most, split=(), kind=jnp.bfloat16):
    entries = width * jax.random.normal(rng, extent, jnp.float32)
    if split:
        entries = entries * levels(rng, extent, split, -0.22, 0.18)
    return jnp.clip(entries, -most, most).astype(kind)


def setup_inputs(seed: int = 0, part: int = 0) -> dict:
    seeds = jax.random.split(jax.random.key(seed), 8)
    own_keys = jax.random.split(jax.random.fold_in(seeds[7], part), 8)
    x_inner = gaussian(own_keys[0], (FRAMES, P_SIZE, E), 1.0, 6.0, ((0, 16),))
    bc_inputs = gaussian(own_keys[1], (FRAMES, P_SIZE, 4 * N), 0.25, 2.0, ((0, 16),))
    step_raw = gaussian(own_keys[2], (FRAMES, P_SIZE, 2 * H), 1.0, 5.0, ((0, 16),))
    decay_rate = jnp.clip(jnp.exp(jax.random.uniform(seeds[3], (2, H), jnp.float32, math.log(0.002), math.log(0.3))), 0.002, 0.3)
    skip_gain = jnp.clip(1.0 + 0.18 * jax.random.normal(seeds[4], (H,), jnp.float32), 0.1, 1.9)
    w_out = gaussian(seeds[5], (E, D), E ** -0.5, 0.125, ((0, 16),))
    grad_out = gaussian(own_keys[6], (FRAMES, P_SIZE, D), 1.0, 6.0, ((0, 16),))
    return dict(x_inner=x_inner, bc_inputs=bc_inputs, step_raw=step_raw, decay_rate=decay_rate, skip_gain=skip_gain, w_out=w_out, grad_out=grad_out)


HIGH = lax.Precision.HIGHEST

def block_scan(heads_in, b_rows, c_rows, step_size, decay_rates, block_len):
    length, nheads, head_dim = heads_in.shape
    block_count = length // block_len
    state_size = b_rows.shape[-1]
    x_blocks = heads_in.reshape(block_count, block_len, nheads, head_dim)
    b_blocks = b_rows.reshape(block_count, block_len, state_size)
    c_blocks = c_rows.reshape(block_count, block_len, state_size)
    s_blocks = step_size.reshape(block_count, block_len, nheads)
    log_cum = jnp.cumsum(-s_blocks * decay_rates, axis=1)
    log_gaps = log_cum[:, :, None, :] - log_cum[:, None, :, :]
    lower_mask = jnp.arange(block_len)[:, None] >= jnp.arange(block_len)[None, :]
    decay_mat = jnp.exp(jnp.where(lower_mask[None, :, :, None], log_gaps, -jnp.inf))
    gram_mat = jnp.einsum('kin,kjn->kij', c_blocks, b_blocks, precision=HIGH)
    weights = gram_mat[:, :, :, None] * decay_mat * s_blocks[:, None, :, :]
    inside = jnp.einsum('kijh,kjhd->kihd', weights, x_blocks, precision=HIGH)
    log_last = log_cum[:, -1, :]
    tail_weight = jnp.exp(log_last[:, None, :] - log_cum) * s_blocks
    states = jnp.einsum('kjh,kjhd,kjn->khdn', tail_weight, x_blocks, b_blocks, precision=HIGH)

    def advance(state_carry, inputs):
        log_end, added_state = inputs
        return (jnp.exp(log_end)[:, None, None] * state_carry + added_state, state_carry)
    final_state, entering = lax.scan(advance, jnp.zeros(states.shape[1:], states.dtype), (log_last, states))
    outside = jnp.einsum('kin,khdn->kihd', c_blocks, entering, precision=HIGH) * jnp.exp(log_cum)[:, :, :, None]
    return (inside + outside).reshape(length, nheads, head_dim)

def whole_scan(heads_in, b_rows, c_rows, step_size, decay_rates):
    length = heads_in.shape[0]
    log_cum = jnp.cumsum(-step_size * decay_rates, axis=0)
    log_gaps = log_cum[:, None, :] - log_cum[None, :, :]
    lower_mask = jnp.arange(length)[:, None] >= jnp.arange(length)[None, :]
    decay_mat = jnp.exp(jnp.where(lower_mask[:, :, None], log_gaps, -jnp.inf))
    gram_mat = jnp.einsum('in,jn->ij', c_rows, b_rows, precision=HIGH)
    weights = gram_mat[:, :, None] * decay_mat * step_size[None, :, :]
    return jnp.einsum('ijh,jhd->ihd', weights, heads_in, precision=HIGH)

def spatial_mix(x_vals, b_vals, c_vals, raw_vals, decay_rates):
    frames, patches, inner_width = x_vals.shape
    nheads = decay_rates.shape[0]
    step_size = jax.nn.softplus(raw_vals)
    heads_in = x_vals.reshape(frames, patches, nheads, inner_width // nheads)
    block_len = math.gcd(patches, 64)

    def one_frame(x_one, b_one, c_one, s_one):
        return block_scan(x_one, b_one, c_one, s_one, decay_rates, block_len)
    result = jax.vmap(one_frame)(heads_in, b_vals, c_vals, step_size)
    return result.reshape(frames, patches, inner_width)

def temporal_mix(x_vals, b_vals, c_vals, raw_vals, decay_rates, skip_gain):
    frames, patches, inner_width = x_vals.shape
    nheads = decay_rates.shape[0]
    step_size = jax.nn.softplus(raw_vals)
    heads_in = x_vals.reshape(frames, patches, nheads, inner_width // nheads)

    def one_patch(x_one, b_one, c_one, s_one):
        return whole_scan(x_one, b_one, c_one, s_one, decay_rates)
    result = jax.vmap(one_patch, in_axes=1, out_axes=1)(heads_in, b_vals, c_vals, step_size)
    result = result + skip_gain[None, None, :, None] * heads_in
    return result.reshape(frames, patches, inner_width)

def reference(x_inner, bc_inputs, step_raw, decay_rate, skip_gain, w_out, grad_out):
    state_size = bc_inputs.shape[-1] // 4
    nheads = skip_gain.shape[0]
    frames, patches, inner_width = x_inner.shape
    model_width = w_out.shape[1]

    def spatial_fn(x_vals, b_vals, c_vals, raw_vals):
        return spatial_mix(x_vals, b_vals, c_vals, raw_vals, decay_rate[0])

    def temporal_fn(x_vals, b_vals, c_vals, raw_vals):
        return temporal_mix(x_vals, b_vals, c_vals, raw_vals, decay_rate[1], skip_gain)
    spatial_out, spatial_back = jax.vjp(spatial_fn, x_inner.astype(jnp.float32), bc_inputs[:, :, :state_size].astype(jnp.float32), bc_inputs[:, :, state_size:2 * state_size].astype(jnp.float32), step_raw[:, :, :nheads].astype(jnp.float32))
    spatial_bf = lax.optimization_barrier(spatial_out.astype(jnp.bfloat16))
    mixed, temporal_back = jax.vjp(temporal_fn, spatial_bf.astype(jnp.float32), bc_inputs[:, :, 2 * state_size:3 * state_size].astype(jnp.float32), bc_inputs[:, :, 3 * state_size:].astype(jnp.float32), step_raw[:, :, nheads:].astype(jnp.float32))
    mixed_rows = mixed.astype(jnp.bfloat16).reshape(-1, inner_width)
    grad_rows = grad_out.reshape(-1, model_width)
    mixed_out = jnp.dot(mixed_rows, w_out, preferred_element_type=jnp.float32).astype(jnp.bfloat16)
    grad_mixed = lax.dot_general(grad_rows, w_out, (((1,), (1,)), ((), ())), preferred_element_type=jnp.float32)
    grad_mixed = lax.optimization_barrier(grad_mixed.astype(jnp.bfloat16))
    grad_w_out = lax.dot_general(mixed_rows, grad_rows, (((0,), (0,)), ((), ())), preferred_element_type=jnp.float32)
    grad_spatial32, grad_bt, grad_ct, grad_raw_t = temporal_back(grad_mixed.astype(jnp.float32).reshape(frames, patches, inner_width))
    grad_spatial = lax.optimization_barrier(grad_spatial32.astype(jnp.bfloat16))
    grad_x32, grad_bs, grad_cs, grad_raw_s = spatial_back(grad_spatial.astype(jnp.float32))
    grad_bc = jnp.concatenate([grad_bs, grad_cs, grad_bt, grad_ct], axis=-1).astype(jnp.bfloat16)
    grad_step = jnp.concatenate([grad_raw_s, grad_raw_t], axis=-1).astype(jnp.bfloat16)
    return (mixed_out.reshape(frames, patches, model_width), grad_x32.astype(jnp.bfloat16), grad_bc, grad_step, grad_w_out)
```

```python
import jax
import jax.numpy as jnp
from jax import lax
from jax.experimental import pallas as pl
from jax.experimental.pallas import tpu as pltpu
from jax.sharding import PartitionSpec as P

F32 = jnp.float32
BF16 = jnp.bfloat16
LOG2E = 1.4426950408889634
CAP = 8.0

ROWS = 192
HEADS = 32
PAIRS = 16
MODEL = 1024
FRAMES = 16
PATCHES = 12
TILES = MODEL // 128
SENT = PAIRS + TILES + 2
HIGH = lax.Precision.HIGHEST
MIB = 1024 * 1024

SPATIAL_FWD = (((0, 128), (0, 128)), ((128, 192), (0, 192)))
SPATIAL_BWD = (((0, 128), (0, 192)), ((128, 192), (128, 192)))
TEMPORAL = (((0, 128), (0, 128)), ((128, 192), (128, 192)))


def dot(a, b, contract=((1,), (0,)), precision=None):
    return lax.dot_general(
        a, b, (contract, ((), ())), precision=precision, preferred_element_type=F32
    )


def mask_of(temporal, transposed=False):
    i = lax.broadcasted_iota(jnp.int32, (ROWS, ROWS), 1 if transposed else 0)
    j = lax.broadcasted_iota(jnp.int32, (ROWS, ROWS), 0 if transposed else 1)
    keep = i >= j
    if temporal:
        keep = keep & ((i >> 4) == (j >> 4))
    return keep


def softplus(v):
    return jnp.maximum(v, 0.0) + jnp.log1p(jnp.exp(-jnp.abs(v)))


def decay_terms(raw, rate, temporal):
    step = softplus(raw)
    cum = dot(mask_of(temporal).astype(F32), step * rate, precision=HIGH) * (-LOG2E)
    return step, cum, jnp.log(step) * LOG2E - cum


def head_lanes(shape):
    return lax.broadcasted_iota(jnp.int32, shape, 1) < 64


def split_pair(v):
    low = head_lanes(v.shape)
    zero = jnp.zeros_like(v)
    return jnp.where(low, v, zero), jnp.where(low, zero, v)


def both_heads(pair, one_head):
    return jnp.concatenate([one_head(2 * pair), one_head(2 * pair + 1)], axis=0)


def pick_heads(v):
    return jnp.where(head_lanes((ROWS, 128)), v[:ROWS], v[ROWS:])


def padded(parts, block, lanes):
    out = []
    for v, (_, (c0, c1)) in zip(parts, block):
        row = [jnp.zeros((v.shape[0], c0), v.dtype)] if c0 else []
        row.append(v)
        if c1 < lanes:
            row.append(jnp.zeros((v.shape[0], lanes - c1), v.dtype))
        out.append(jnp.concatenate(row, axis=1) if len(row) > 1 else v)
    return jnp.concatenate(out, axis=0)


def scan_forward(blocks, gram, cum, from_row, x_pair, pair):
    def weights(h):
        parts = []
        for (i0, i1), (j0, j1) in blocks:
            e = jnp.exp2(jnp.minimum(cum[i0:i1, h : h + 1] + from_row[h : h + 1, j0:j1], CAP))
            parts.append((e * gram[i0:i1, j0:j1]).astype(BF16))
        return padded(parts, blocks, ROWS)

    return pick_heads(dot(both_heads(pair, weights), x_pair))


def scan_backward(blocks, gram_t, cum_row, from_col, x_pair, dy_pair, pair, dgram, rowsum, colsum):
    products = dot(jnp.concatenate(split_pair(x_pair), axis=0), dy_pair, ((1,), (1,)))
    added = [None] * len(blocks)

    def weights(h):
        parts = []
        sums = []
        for n, ((j0, j1), (i0, i1)) in enumerate(blocks):
            e = jnp.exp2(jnp.minimum(from_col[j0:j1, h : h + 1] + cum_row[h : h + 1, i0:i1], CAP))
            w = e * gram_t[j0:j1, i0:i1]
            base = ROWS * (h - 2 * pair)
            p = products[base + j0 : base + j1, i0:i1]
            t = p * e
            added[n] = t if added[n] is None else added[n] + t
            m = p * w
            colsum[j0:j1, h : h + 1] = jnp.sum(m, axis=1, keepdims=True)
            sums.append((i0, i1, jnp.sum(m, axis=0, keepdims=True)))
            parts.append(w.astype(BF16))
        (a0, a1, first), (b0, b1, second) = sums
        if b0 < a1:
            rowsum[h : h + 1, a0:b0] = first[:, : b0 - a0]
            rowsum[h : h + 1, b0:b1] = first[:, b0 - a0 :] + second
        else:
            rowsum[h : h + 1, a0:a1] = first
            rowsum[h : h + 1, b0:b1] = second
        return padded(parts, blocks, ROWS)

    dx = pick_heads(dot(both_heads(pair, weights), dy_pair))
    for ((j0, j1), (i0, i1)), t in zip(blocks, added):
        dgram[j0:j1, i0:i1] += t
    return dx


def finish_backward(temporal, dgram, rowsum, colsum, b, c, raw, step, rate):
    dg = jnp.where(mask_of(temporal, True), dgram[...], 0.0).astype(BF16)
    db = dot(dg, c)
    dc = dot(dg, b, ((0,), (0,)))
    col = colsum[...]
    dcum = rowsum[...].T - col
    dlog = dot(mask_of(temporal, True).astype(F32), dcum, precision=HIGH)
    dstep = col / step - rate * dlog
    draw = dstep / (1.0 + jnp.exp(-raw))
    return jnp.concatenate([db, dc], axis=1), draw


def put_spatial(wide, row, v):
    wide[pl.ds(row, ROWS, stride=SENT), :] = v


def get_spatial(wide, row):
    return wide[pl.ds(row, ROWS, stride=SENT), :]


def put_temporal(wide, row, v):
    for p in range(PATCHES):
        wide[pl.ds(p * SENT + row, FRAMES, stride=PATCHES * SENT), :] = v[16 * p : 16 * p + 16]


def get_temporal(wide, row):
    return jnp.concatenate(
        [wide[pl.ds(p * SENT + row, FRAMES, stride=PATCHES * SENT), :] for p in range(PATCHES)], axis=0
    )


def spatial_forward_kernel(
    x_hbm, bc_hbm, raw_hbm, grad_hbm, rate_ref, out_ref, wide, x_ref, bc_ref, raw_ref, grad_ref, sems
):
    def load(n, src, dst):
        copy = pltpu.make_async_copy(src, dst, sems.at[n])
        copy.start()
        return copy

    maps = load(0, bc_hbm, bc_ref)
    steps = load(1, raw_hbm, raw_ref)
    quarters = [pl.ds(512 * q, 512) for q in range(4)]
    xs = [load(2 + q, x_hbm.at[:, quarters[q]], x_ref.at[:, quarters[q]]) for q in range(4)]
    grads = load(6, grad_hbm, grad_ref)
    steps.wait()
    raw = raw_ref[...].astype(F32).T
    put_spatial(wide, PAIRS + TILES + 1, jnp.concatenate([raw, jnp.zeros_like(raw)], axis=1))
    _, cum, from_col = decay_terms(raw[:, :HEADS], rate_ref[0:1, :], False)
    from_row = from_col.T
    maps.wait()
    put_spatial(wide, PAIRS + TILES, bc_ref[:, 128:].astype(F32))
    gram = dot(bc_ref[:, 64:128], bc_ref[:, 0:64], ((1,), (1,)))
    gram = jnp.where(mask_of(False), gram, 0.0)
    for g in range(PAIRS):
        if g % 4 == 0:
            xs[g // 4].wait()
        y = scan_forward(SPATIAL_FWD, gram, cum, from_row, x_ref[:, 128 * g : 128 * g + 128], g)
        put_spatial(wide, g, y)
    grads.wait()
    for k in range(TILES):
        put_spatial(wide, PAIRS + k, grad_ref[:, 128 * k : 128 * k + 128].astype(F32))
    out_ref[...] = wide[...].astype(BF16)


def weight_grad(mixed_ref, grad_ref, parity, column):
    lanes = [pl.ds(pl.multiple_of((2 * z + parity) * 128, 128), 128) for z in range(PAIRS // 2)]
    rows = jnp.concatenate([mixed_ref[:, at] for at in lanes], axis=1)
    return dot(rows, grad_ref[:, column : column + 256], ((0,), (0,)))


def temporal_forward_kernel(
    core_ref, here_ref, rate_ref, gain_ref,
    x_out, mixed_out, grad_out, bc_out, raw_out, other_out,
    wide, x_ref, mixed_ref, grad_ref, bc_ref, raw_ref, other_ref, sems,
):
    saves = []

    def save(src, dst):
        copy = pltpu.make_async_copy(src, dst, sems.at[len(saves)])
        copy.start()
        saves.append(copy)

    wide[...] = here_ref[...].astype(F32)
    for k in range(TILES):
        grad_ref[:, 128 * k : 128 * k + 128] = get_temporal(wide, PAIRS + k).astype(BF16)
    save(grad_ref, grad_out)
    bc = get_temporal(wide, PAIRS + TILES).astype(BF16)
    bc_ref[...] = bc
    save(bc_ref, bc_out)
    raw = get_temporal(wide, PAIRS + TILES + 1)
    raw_ref[...] = raw
    save(raw_ref, raw_out)
    _, cum, from_col = decay_terms(raw[:, HEADS : 2 * HEADS], rate_ref[1:2, :], True)
    from_row = from_col.T
    gram = dot(bc[:, 64:128], bc[:, 0:64], ((1,), (1,)))
    gram = jnp.where(mask_of(True), gram, 0.0)
    low = head_lanes((1, 128))
    for g in range(PAIRS):
        x = get_temporal(wide, g)
        xb = x.astype(BF16)
        x_ref[:, 128 * g : 128 * g + 128] = xb
        y = scan_forward(TEMPORAL, gram, cum, from_row, xb, g)
        gain = jnp.where(low, gain_ref[0, 2 * g], gain_ref[0, 2 * g + 1])
        mixed_ref[:, 128 * g : 128 * g + 128] = (y + gain * x).astype(BF16)
    save(x_ref, x_out)
    save(mixed_ref, mixed_out)
    for column in range(0, MODEL, 256):
        dw = weight_grad(mixed_ref, grad_ref, 1 - core_ref[0], column)
        other_ref[:, :, column : column + 256] = dw.reshape(8, 128, 256).astype(BF16)
    save(other_ref, other_out)
    for copy in saves:
        copy.wait()


def weight_grad_kernel(
    core_ref, mixed_hbm, grad_hbm, got_ref, back_in, out_ref, back_out, mixed_ref, grad_ref, sems
):
    del back_in, back_out
    loads = [
        pltpu.make_async_copy(mixed_hbm, mixed_ref, sems.at[0]),
        pltpu.make_async_copy(grad_hbm, grad_ref, sems.at[1]),
    ]
    for copy in loads:
        copy.start()
    for copy in loads:
        copy.wait()
    for column in range(0, MODEL, 256):
        at = slice(column, column + 256)
        dw = weight_grad(mixed_ref, grad_ref, core_ref[0], column).reshape(8, 128, 256)
        out_ref[:, :, at] = (dw + got_ref[:, :, at].astype(F32)).astype(BF16)


def temporal_backward_kernel(
    place_ref, x_hbm, mixed_hbm, grad_hbm, bc_hbm, raw_hbm, mine_hbm, theirs_hbm, rate_ref, gain_ref,
    out_ref, wide, weight, dy_all, x_ref, mixed_ref, grad_ref, bc_ref, raw_ref,
    dgram, rowsum, colsum, sems,
):
    core, x, y = place_ref[0], place_ref[1], place_ref[2]
    pairs = [
        (raw_hbm, raw_ref),
        (bc_hbm, bc_ref),
        (grad_hbm, grad_ref),
        (x_hbm, x_ref),
        (mixed_hbm, mixed_ref),
    ]
    for src, half in ((mine_hbm, core), (theirs_hbm, 1 - core)):
        for a in range(4):
            for b in range(4):
                from_x = x ^ (a + half * (b - a))
                from_y = y ^ (b + half * (a - b))
                at = pl.ds(pl.multiple_of(256 * from_y, 256), 256)
                pairs.append((src.at[a, b], weight.at[:, half, from_x, :, at]))
    loads = [pltpu.make_async_copy(src, dst, sems.at[n]) for n, (src, dst) in enumerate(pairs)]
    for copy in loads:
        copy.start()
    loads[0].wait()
    raw = raw_ref[:, HEADS : 2 * HEADS]
    rate = rate_ref[1:2, :]
    step, cum, from_col = decay_terms(raw, rate, True)
    cum_row = cum.T
    loads[1].wait()
    b, c = bc_ref[:, 0:64], bc_ref[:, 64:128]
    gram_t = jnp.where(mask_of(True, True), dot(b, c, ((1,), (1,))), 0.0)
    dgram[...] = jnp.zeros_like(dgram)
    low = head_lanes((1, 128))
    for copy in loads[2:]:
        copy.wait()
    for z in range(PAIRS // 2):
        w = weight[2 * z : 2 * z + 2].reshape(256, MODEL)
        dy_all[:, 256 * z : 256 * z + 256] = dot(grad_ref[...], w, ((1,), (1,))).astype(BF16)
    for g in range(PAIRS):
        dy = dy_all[:, 128 * g : 128 * g + 128]
        dx = scan_backward(
            TEMPORAL, gram_t, cum_row, from_col, x_ref[:, 128 * g : 128 * g + 128], dy, g,
            dgram, rowsum, colsum,
        )
        gain = jnp.where(low, gain_ref[0, 2 * g], gain_ref[0, 2 * g + 1])
        put_temporal(wide, g, dx + gain * dy.astype(F32))
    dbc, draw = finish_backward(True, dgram, rowsum, colsum, b, c, raw, step, rate)
    put_temporal(wide, PAIRS + TILES, dbc)
    put_temporal(
        wide, PAIRS + TILES + 1, jnp.concatenate([draw, jnp.zeros((ROWS, 128 - HEADS), F32)], axis=1)
    )
    for k in range(0, TILES, 2):
        w = weight[:, :, :, :, 128 * k : 128 * k + 256].reshape(2048, 256)
        projected = dot(mixed_ref[...], w)
        for t in range(2):
            put_temporal(wide, PAIRS + k + t, projected[:, 128 * t : 128 * t + 128])
    out_ref[...] = wide[...].astype(BF16)


def spatial_backward_kernel(
    x_ref, back_ref, bc_ref, raw_ref, rate_ref, out_ref, dx_ref, dbc_ref, draw_ref,
    wide, dgram, rowsum, colsum,
):
    wide[...] = back_ref[...].astype(F32)
    for k in range(TILES):
        out_ref[:, 128 * k : 128 * k + 128] = get_spatial(wide, PAIRS + k).astype(BF16)
    raw = raw_ref[...].astype(F32).T[:, :HEADS]
    rate = rate_ref[0:1, :]
    step, cum, from_col = decay_terms(raw, rate, False)
    cum_row = cum.T
    b, c = bc_ref[:, 0:64], bc_ref[:, 64:128]
    gram_t = jnp.where(mask_of(False, True), dot(b, c, ((1,), (1,))), 0.0)
    dgram[...] = jnp.zeros_like(dgram)
    for g in range(PAIRS):
        dy = get_spatial(wide, g).astype(BF16)
        dx = scan_backward(
            SPATIAL_BWD, gram_t, cum_row, from_col, x_ref[:, 128 * g : 128 * g + 128], dy, g,
            dgram, rowsum, colsum,
        )
        dx_ref[:, 128 * g : 128 * g + 128] = dx.astype(BF16)
    dbc, draw = finish_backward(False, dgram, rowsum, colsum, b, c, raw, step, rate)
    dbc_ref[:, 0:128] = dbc.astype(BF16)
    dbc_ref[:, 128:256] = get_spatial(wide, PAIRS + TILES).astype(BF16)
    draw_t = get_spatial(wide, PAIRS + TILES + 1)
    draw_ref[...] = jnp.concatenate([draw, draw_t[:, :HEADS]], axis=1).T.astype(BF16)


def shape(*dims, dtype=BF16):
    return jax.ShapeDtypeStruct(dims, dtype)


def scan_scratch():
    return [
        pltpu.VMEM((ROWS, ROWS), F32),
        pltpu.VMEM((HEADS, ROWS), F32),
        pltpu.VMEM((ROWS, HEADS), F32),
    ]


def smem():
    return pl.BlockSpec(memory_space=pltpu.SMEM)


def vmem(n):
    return [pl.BlockSpec(memory_space=pltpu.VMEM)] * n


def exchange(v):
    blocks = v.reshape(16, v.shape[0] // 16, 128)
    return lax.all_to_all(blocks, "tm", 0, 0, tiled=True).reshape(v.shape)


def hbm(n):
    return [pl.BlockSpec(memory_space=pltpu.HBM)] * n


def call(kernel, outs, in_specs, scratch, us, mib, out_specs=None, aliases={}):
    more = {} if out_specs is None else {"out_specs": tuple(out_specs)}
    return pl.pallas_call(
        kernel,
        **more,
        input_output_aliases=aliases,
        out_shape=outs,
        in_specs=in_specs,
        scratch_shapes=scratch,
        compiler_params=pltpu.CompilerParams(vmem_limit_bytes=mib * MIB),
        cost_estimate=pl.CostEstimate(
            flops=int(us * 1.0e9), bytes_accessed=int(us * 3.0e6), transcendentals=0
        ),
    )


def across(axis, v, bit):
    return lax.ppermute(v, axis, [(s, s ^ bit) for s in range(16)])


def in_hbm(*arrays):
    return [pltpu.with_memory_space_constraint(v, pltpu.HBM) for v in arrays]


def pass_kernel(v_in, token, v_out):
    del v_in, token, v_out


def after(v, token):
    return pl.pallas_call(
        pass_kernel,
        out_shape=pltpu.HBM(v.shape, v.dtype),
        in_specs=hbm(2),
        out_specs=hbm(1)[0],
        input_output_aliases={0: 0},
    )(*in_hbm(v, token))


def weight_part(w_out):
    clip = lax.axis_index("clip")
    mine = lax.dynamic_slice(
        w_out.reshape(2, 64, MODEL), (0, 16 * (clip // 4), 256 * lax.rem(clip, 4)), (2, 16, 256)
    )
    return lax.all_to_all(jnp.tile(mine, (8, 1, 1)), "tm", 0, 0, tiled=True)


def gather_weight(part):
    for step in range(2):
        got = [part]
        for bits in (1, 2, 3):
            to = []
            for device in range(256):
                along_x = (device % 2) != step
                to.append((device, device ^ ((bits * 64) if along_x else (bits * 16))))
            got.append(lax.ppermute(part, ("clip", "tm"), to))
        part = jnp.stack(got)
    return part, across("tm", part, 1)


def on_device(x_inner, bc_inputs, step_raw, decay_rate, skip_gain, w_out, grad_out):
    x, bc, grad = x_inner[0], bc_inputs[0], grad_out[0]
    raw = step_raw[0].T
    gain = skip_gain.reshape(1, HEADS)
    tm, clip = lax.axis_index("tm"), lax.axis_index("clip")
    core = jnp.stack([lax.rem(tm, 2), clip // 4, lax.rem(clip, 4)]).astype(jnp.int32)
    along_z = [[2 * z + c for z in range(8)] for c in range(2)]
    wide = pltpu.VMEM((ROWS * SENT, 128), F32)

    part = weight_part(w_out)
    ahead = call(
        spatial_forward_kernel,
        shape(ROWS * SENT, 128),
        hbm(4) + vmem(1),
        [
            wide,
            pltpu.VMEM((ROWS, 2048), BF16),
            pltpu.VMEM((ROWS, 256), BF16),
            pltpu.VMEM((2 * HEADS, ROWS), BF16),
            pltpu.VMEM((ROWS, MODEL), BF16),
            pltpu.SemaphoreType.DMA((7,)),
        ],
        4,
        16,
    )(*in_hbm(x, bc, raw, grad), decay_rate)
    mine, theirs = gather_weight(after(part, ahead))
    ahead = exchange(ahead)

    kept = [(ROWS, 2048), (ROWS, 2048), (ROWS, MODEL), (ROWS, 128), (ROWS, 128), (8, 128, MODEL)]
    types = [BF16, BF16, BF16, BF16, F32, BF16]
    x_t, mixed, grad_t, bc_t, raw_t, other = call(
        temporal_forward_kernel,
        tuple(pltpu.HBM(dims, dtype) for dims, dtype in zip(kept, types)),
        [smem()] + vmem(2) + [smem()],
        [wide]
        + [pltpu.VMEM(dims, dtype) for dims, dtype in zip(kept, types)]
        + [pltpu.SemaphoreType.DMA((6,))],
        4,
        20,
        out_specs=hbm(6),
    )(core, ahead, decay_rate, gain)

    got = across("tm", other, 1)
    back = call(
        temporal_backward_kernel,
        shape(ROWS * SENT, 128),
        [smem()] + hbm(7) + vmem(1) + [smem()],
        [wide, pltpu.VMEM((16, 2, 4, 16, MODEL), BF16), pltpu.VMEM((ROWS, 2048), BF16)]
        + [pltpu.VMEM(dims, dtype) for dims, dtype in zip(kept[:5], types)]
        + scan_scratch()
        + [pltpu.SemaphoreType.DMA((37,))],
        7,
        24,
    )(core, *in_hbm(x_t, mixed, grad_t, bc_t, raw_t, mine, theirs), decay_rate, gain)

    partial, back = call(
        weight_grad_kernel,
        (shape(8, 128, MODEL), pltpu.HBM((ROWS * SENT, 128), BF16)),
        [smem()] + hbm(2) + vmem(1) + hbm(1),
        [pltpu.VMEM((ROWS, 2048), BF16), pltpu.VMEM((ROWS, MODEL), BF16), pltpu.SemaphoreType.DMA((2,))],
        2,
        14,
        out_specs=vmem(1) + hbm(1),
        aliases={4: 1},
    )(core, *in_hbm(mixed, grad_t), got, *in_hbm(back))
    grad_w = lax.psum_scatter(
        partial, "tm", scatter_dimension=0, axis_index_groups=along_z, tiled=False
    )
    back = exchange(back)

    mixed_out, grad_x, grad_bc, grad_step = call(
        spatial_backward_kernel,
        (shape(ROWS, MODEL), shape(ROWS, 2048), shape(ROWS, 256), shape(2 * HEADS, ROWS)),
        vmem(5),
        [wide] + scan_scratch(),
        8,
        18,
    )(x, back, bc, raw, decay_rate)
    return (mixed_out[None], grad_x[None], grad_bc[None], grad_step.T[None], grad_w.astype(F32))


def solution(mesh):
    rows = P(("clip", "tm"), None, None)
    return jax.shard_map(
        on_device,
        mesh=mesh,
        in_specs=(rows, rows, rows, P(), P(), P("tm", None), rows),
        out_specs=(rows, rows, rows, rows, P(("clip", "tm"), None)),
        check_vma=False,
    )
```

```python
import jax
import jax.numpy as jnp
from jax import lax
from jax.experimental import pallas as pl
from jax.experimental.pallas import tpu as pltpu
from jax.sharding import PartitionSpec as P

F32 = jnp.float32
BF16 = jnp.bfloat16
LOG2E = 1.4426950408889634
CAP = 8.0

ROWS = 192
HEADS = 32
PAIRS = 16
MODEL = 1024
FRAMES = 16
PATCHES = 12
TILES = MODEL // 128
SENT = PAIRS + TILES + 2
HIGH = lax.Precision.HIGHEST
MIB = 1024 * 1024

SPATIAL_FWD = (((0, 128), (0, 128)), ((128, 192), (0, 192)))
SPATIAL_BWD = (((0, 128), (0, 192)), ((128, 192), (128, 192)))
TEMPORAL = (((0, 128), (0, 128)), ((128, 192), (128, 192)))


def dot(a, b, contract=((1,), (0,)), precision=None):
    return lax.dot_general(
        a, b, (contract, ((), ())), precision=precision, preferred_element_type=F32
    )


def mask_of(temporal, transposed=False):
    i = lax.broadcasted_iota(jnp.int32, (ROWS, ROWS), 1 if transposed else 0)
    j = lax.broadcasted_iota(jnp.int32, (ROWS, ROWS), 0 if transposed else 1)
    keep = i >= j
    if temporal:
        keep = keep & ((i >> 4) == (j >> 4))
    return keep


def softplus(v):
    return jnp.maximum(v, 0.0) + jnp.log1p(jnp.exp(-jnp.abs(v)))


def decay_terms(raw, rate, temporal):
    step = softplus(raw)
    cum = dot(mask_of(temporal).astype(F32), step * rate, precision=HIGH) * (-LOG2E)
    return step, cum, jnp.log(step) * LOG2E - cum


def head_lanes(shape):
    return lax.broadcasted_iota(jnp.int32, shape, 1) < 64


def split_pair(v):
    low = head_lanes(v.shape)
    zero = jnp.zeros_like(v)
    return jnp.where(low, v, zero), jnp.where(low, zero, v)


def both_heads(pair, one_head):
    return jnp.concatenate([one_head(2 * pair), one_head(2 * pair + 1)], axis=0)


def pick_heads(v):
    return jnp.where(head_lanes((ROWS, 128)), v[:ROWS], v[ROWS:])


def padded(parts, block, lanes):
    out = []
    for v, (_, (c0, c1)) in zip(parts, block):
        row = [jnp.zeros((v.shape[0], c0), v.dtype)] if c0 else []
        row.append(v)
        if c1 < lanes:
            row.append(jnp.zeros((v.shape[0], lanes - c1), v.dtype))
        out.append(jnp.concatenate(row, axis=1) if len(row) > 1 else v)
    return jnp.concatenate(out, axis=0)


def scan_forward(blocks, gram, cum, from_row, x_pair, pair):
    def weights(h):
        parts = []
        for (i0, i1), (j0, j1) in blocks:
            e = jnp.exp2(jnp.minimum(cum[i0:i1, h : h + 1] + from_row[h : h + 1, j0:j1], CAP))
            parts.append((e * gram[i0:i1, j0:j1]).astype(BF16))
        return padded(parts, blocks, ROWS)

    return pick_heads(dot(both_heads(pair, weights), x_pair))


def scan_backward(
    blocks, gram_t, cum_row, from_col, x_pair, dy_pair, pair, dgram, rowsum, colsum=None, by_x=None
):
    products = dot(jnp.concatenate(split_pair(x_pair), axis=0), dy_pair, ((1,), (1,)))
    added = [None] * len(blocks)

    def weights(h):
        parts = []
        sums = []
        for n, ((j0, j1), (i0, i1)) in enumerate(blocks):
            e = jnp.exp2(jnp.minimum(from_col[j0:j1, h : h + 1] + cum_row[h : h + 1, i0:i1], CAP))
            w = e * gram_t[j0:j1, i0:i1]
            rounded = w.astype(BF16)
            if colsum is None:
                w = rounded.astype(F32)
            base = ROWS * (h - 2 * pair)
            p = products[base + j0 : base + j1, i0:i1]
            t = p * e
            added[n] = t if added[n] is None else added[n] + t
            m = p * w
            if colsum is not None:
                colsum[j0:j1, h : h + 1] = jnp.sum(m, axis=1, keepdims=True)
            sums.append((i0, i1, jnp.sum(m, axis=0, keepdims=True)))
            parts.append(rounded)
        (a0, a1, first), (b0, b1, second) = sums
        if b0 < a1:
            rowsum[h : h + 1, a0:b0] = first[:, : b0 - a0]
            rowsum[h : h + 1, b0:b1] = first[:, b0 - a0 :] + second
        else:
            rowsum[h : h + 1, a0:a1] = first
            rowsum[h : h + 1, b0:b1] = second
        return padded(parts, blocks, ROWS)

    dx = pick_heads(dot(both_heads(pair, weights), dy_pair))
    if colsum is None:
        by_x[:, 128 * pair : 128 * pair + 128] = dx * x_pair.astype(F32)
    for ((j0, j1), (i0, i1)), t in zip(blocks, added):
        dgram[j0:j1, i0:i1] += t
    return dx


def head_sums(v):
    lane = lax.broadcasted_iota(jnp.int32, (2048, 128), 0)
    head = lax.broadcasted_iota(jnp.int32, (2048, 128), 1)
    ones = ((lane >> 6) == head).astype(BF16)
    high = v.astype(BF16)
    rest = (v - high.astype(F32)).astype(BF16)
    both = dot(jnp.concatenate([high, rest], axis=0), ones)
    return (both[:ROWS] + both[ROWS:])[:, :HEADS]


def finish_backward(temporal, dgram, rowsum, col, b, c, raw, step, rate):
    dg = jnp.where(mask_of(temporal, True), dgram[...], 0.0).astype(BF16)
    db = dot(dg, c)
    dc = dot(dg, b, ((0,), (0,)))
    dcum = rowsum[...].T - col
    dlog = dot(mask_of(temporal, True).astype(F32), dcum, precision=HIGH)
    dstep = col / step - rate * dlog
    draw = dstep / (1.0 + jnp.exp(-raw))
    return jnp.concatenate([db, dc], axis=1), draw


def put_spatial(wide, row, v):
    wide[pl.ds(row, ROWS, stride=SENT), :] = v


def get_spatial(wide, row):
    return wide[pl.ds(row, ROWS, stride=SENT), :]


def put_temporal(wide, row, v):
    for p in range(PATCHES):
        wide[pl.ds(p * SENT + row, FRAMES, stride=PATCHES * SENT), :] = v[16 * p : 16 * p + 16]


def get_temporal(wide, row):
    return jnp.concatenate(
        [wide[pl.ds(p * SENT + row, FRAMES, stride=PATCHES * SENT), :] for p in range(PATCHES)], axis=0
    )


def spatial_forward_kernel(
    x_hbm, bc_hbm, raw_hbm, grad_hbm, rate_ref, out_ref, wide, x_ref, bc_ref, raw_ref, grad_ref, sems
):
    def load(n, src, dst):
        copy = pltpu.make_async_copy(src, dst, sems.at[n])
        copy.start()
        return copy

    maps = load(0, bc_hbm, bc_ref)
    steps = load(1, raw_hbm, raw_ref)
    quarters = [pl.ds(512 * q, 512) for q in range(4)]
    xs = [load(2 + q, x_hbm.at[:, quarters[q]], x_ref.at[:, quarters[q]]) for q in range(4)]
    grads = load(6, grad_hbm, grad_ref)
    steps.wait()
    raw = raw_ref[...].astype(F32).T
    put_spatial(wide, PAIRS + TILES + 1, jnp.concatenate([raw, jnp.zeros_like(raw)], axis=1))
    _, cum, from_col = decay_terms(raw[:, :HEADS], rate_ref[0:1, :], False)
    from_row = from_col.T
    maps.wait()
    put_spatial(wide, PAIRS + TILES, bc_ref[:, 128:].astype(F32))
    gram = dot(bc_ref[:, 64:128], bc_ref[:, 0:64], ((1,), (1,)))
    gram = jnp.where(mask_of(False), gram, 0.0)
    for g in range(PAIRS):
        if g % 4 == 0:
            xs[g // 4].wait()
        y = scan_forward(SPATIAL_FWD, gram, cum, from_row, x_ref[:, 128 * g : 128 * g + 128], g)
        put_spatial(wide, g, y)
    grads.wait()
    for k in range(TILES):
        put_spatial(wide, PAIRS + k, grad_ref[:, 128 * k : 128 * k + 128].astype(F32))
    out_ref[...] = wide[...].astype(BF16)


def weight_grad(mixed_ref, grad_ref, parity, column):
    lanes = [pl.ds(pl.multiple_of((2 * z + parity) * 128, 128), 128) for z in range(PAIRS // 2)]
    rows = jnp.concatenate([mixed_ref[:, at] for at in lanes], axis=1)
    return dot(rows, grad_ref[:, column : column + 256], ((0,), (0,)))


def temporal_forward_kernel(
    core_ref, here_ref, rate_ref, gain_ref,
    x_out, mixed_out, grad_out, bc_out, raw_out, other_out,
    wide, x_ref, mixed_ref, grad_ref, bc_ref, raw_ref, other_ref, sems,
):
    saves = []

    def save(src, dst):
        copy = pltpu.make_async_copy(src, dst, sems.at[len(saves)])
        copy.start()
        saves.append(copy)

    wide[...] = here_ref[...].astype(F32)
    for k in range(TILES):
        grad_ref[:, 128 * k : 128 * k + 128] = get_temporal(wide, PAIRS + k).astype(BF16)
    save(grad_ref, grad_out)
    bc = get_temporal(wide, PAIRS + TILES).astype(BF16)
    bc_ref[...] = bc
    save(bc_ref, bc_out)
    raw = get_temporal(wide, PAIRS + TILES + 1)
    raw_ref[...] = raw
    save(raw_ref, raw_out)
    _, cum, from_col = decay_terms(raw[:, HEADS : 2 * HEADS], rate_ref[1:2, :], True)
    from_row = from_col.T
    gram = dot(bc[:, 64:128], bc[:, 0:64], ((1,), (1,)))
    gram = jnp.where(mask_of(True), gram, 0.0)
    low = head_lanes((1, 128))
    for g in range(PAIRS):
        x = get_temporal(wide, g)
        xb = x.astype(BF16)
        x_ref[:, 128 * g : 128 * g + 128] = xb
        y = scan_forward(TEMPORAL, gram, cum, from_row, xb, g)
        gain = jnp.where(low, gain_ref[0, 2 * g], gain_ref[0, 2 * g + 1])
        mixed_ref[:, 128 * g : 128 * g + 128] = (y + gain * x).astype(BF16)
        if g % 4 == 3:
            at = pl.ds(128 * (g - 3), 512)
            save(x_ref.at[:, at], x_out.at[:, at])
            save(mixed_ref.at[:, at], mixed_out.at[:, at])
    for column in range(0, MODEL, 256):
        dw = weight_grad(mixed_ref, grad_ref, 1 - core_ref[0], column)
        at = pl.ds(column, 256)
        other_ref[:, :, at] = dw.reshape(8, 128, 256).astype(BF16)
        save(other_ref.at[:, :, at], other_out.at[:, :, at])
    for copy in saves:
        copy.wait()


def weight_grad_kernel(
    core_ref, mixed_hbm, grad_hbm, got_ref, out_hbm, mixed_ref, grad_ref, out_ref, sems
):
    loads = [
        pltpu.make_async_copy(mixed_hbm, mixed_ref, sems.at[0]),
        pltpu.make_async_copy(grad_hbm, grad_ref, sems.at[1]),
    ]
    for copy in loads:
        copy.start()
    for copy in loads:
        copy.wait()
    saves = []
    for n in range(MODEL // 256):
        at = pl.ds(256 * n, 256)
        dw = weight_grad(mixed_ref, grad_ref, core_ref[0], 256 * n).reshape(8, 128, 256)
        out_ref[:, :, at] = (dw + got_ref[:, :, at].astype(F32)).astype(BF16)
        saves.append(pltpu.make_async_copy(out_ref.at[:, :, at], out_hbm.at[:, :, at], sems.at[2 + n]))
        saves[-1].start()
    for copy in saves:
        copy.wait()


def temporal_backward_kernel(
    place_ref, x_hbm, mixed_hbm, grad_hbm, bc_hbm, raw_hbm, mine_hbm, theirs_hbm, rate_ref, gain_ref,
    out_ref, wide, weight, dy_all, x_ref, mixed_ref, grad_ref, bc_ref, raw_ref,
    dgram, rowsum, colsum, sems,
):
    core, x, y = place_ref[0], place_ref[1], place_ref[2]
    pairs = [
        (raw_hbm, raw_ref),
        (bc_hbm, bc_ref),
        (grad_hbm, grad_ref),
        (x_hbm, x_ref),
        (mixed_hbm, mixed_ref),
    ]
    for src, half in ((mine_hbm, core), (theirs_hbm, 1 - core)):
        for a in range(4):
            for b in range(4):
                from_x = x ^ (a + half * (b - a))
                from_y = y ^ (b + half * (a - b))
                at = pl.ds(pl.multiple_of(256 * from_y, 256), 256)
                pairs.append((src.at[a, b], weight.at[:, half, from_x, :, at]))
    loads = [pltpu.make_async_copy(src, dst, sems.at[n]) for n, (src, dst) in enumerate(pairs)]
    for copy in loads:
        copy.start()
    loads[0].wait()
    raw = raw_ref[:, HEADS : 2 * HEADS]
    rate = rate_ref[1:2, :]
    step, cum, from_col = decay_terms(raw, rate, True)
    cum_row = cum.T
    loads[1].wait()
    b, c = bc_ref[:, 0:64], bc_ref[:, 64:128]
    gram_t = jnp.where(mask_of(True, True), dot(b, c, ((1,), (1,))), 0.0)
    dgram[...] = jnp.zeros_like(dgram)
    low = head_lanes((1, 128))
    for copy in loads[2:]:
        copy.wait()
    for z in range(PAIRS // 2):
        w = weight[2 * z : 2 * z + 2].reshape(256, MODEL)
        dy_all[:, 256 * z : 256 * z + 256] = dot(grad_ref[...], w, ((1,), (1,))).astype(BF16)
    for g in range(PAIRS):
        dy = dy_all[:, 128 * g : 128 * g + 128]
        dx = scan_backward(
            TEMPORAL, gram_t, cum_row, from_col, x_ref[:, 128 * g : 128 * g + 128], dy, g,
            dgram, rowsum, colsum,
        )
        gain = jnp.where(low, gain_ref[0, 2 * g], gain_ref[0, 2 * g + 1])
        put_temporal(wide, g, dx + gain * dy.astype(F32))
    dbc, draw = finish_backward(True, dgram, rowsum, colsum[...], b, c, raw, step, rate)
    put_temporal(wide, PAIRS + TILES, dbc)
    put_temporal(
        wide, PAIRS + TILES + 1, jnp.concatenate([draw, jnp.zeros((ROWS, 128 - HEADS), F32)], axis=1)
    )
    for k in range(0, TILES, 2):
        w = weight[:, :, :, :, 128 * k : 128 * k + 256].reshape(2048, 256)
        projected = dot(mixed_ref[...], w)
        for t in range(2):
            put_temporal(wide, PAIRS + k + t, projected[:, 128 * t : 128 * t + 128])
    out_ref[...] = wide[...].astype(BF16)


def spatial_backward_kernel(
    x_ref, back_ref, bc_ref, raw_ref, rate_ref, out_ref, dx_ref, dbc_ref, draw_ref,
    wide, dgram, rowsum, by_x,
):
    wide[...] = back_ref[...].astype(F32)
    for k in range(TILES):
        out_ref[:, 128 * k : 128 * k + 128] = get_spatial(wide, PAIRS + k).astype(BF16)
    raw = raw_ref[...].astype(F32).T[:, :HEADS]
    rate = rate_ref[0:1, :]
    step, cum, from_col = decay_terms(raw, rate, False)
    cum_row = cum.T
    b, c = bc_ref[:, 0:64], bc_ref[:, 64:128]
    gram_t = jnp.where(mask_of(False, True), dot(b, c, ((1,), (1,))), 0.0)
    dgram[...] = jnp.zeros_like(dgram)
    for g in range(PAIRS):
        dy = get_spatial(wide, g).astype(BF16)
        dx = scan_backward(
            SPATIAL_BWD, gram_t, cum_row, from_col, x_ref[:, 128 * g : 128 * g + 128], dy, g,
            dgram, rowsum, by_x=by_x,
        )
        dx_ref[:, 128 * g : 128 * g + 128] = dx.astype(BF16)
    dbc, draw = finish_backward(False, dgram, rowsum, head_sums(by_x[...]), b, c, raw, step, rate)
    dbc_ref[:, 0:128] = dbc.astype(BF16)
    dbc_ref[:, 128:256] = get_spatial(wide, PAIRS + TILES).astype(BF16)
    draw_t = get_spatial(wide, PAIRS + TILES + 1)
    draw_ref[...] = jnp.concatenate([draw, draw_t[:, :HEADS]], axis=1).T.astype(BF16)


def shape(*dims, dtype=BF16):
    return jax.ShapeDtypeStruct(dims, dtype)


def scan_scratch():
    return [
        pltpu.VMEM((ROWS, ROWS), F32),
        pltpu.VMEM((HEADS, ROWS), F32),
        pltpu.VMEM((ROWS, HEADS), F32),
    ]


def smem():
    return pl.BlockSpec(memory_space=pltpu.SMEM)


def vmem(n):
    return [pl.BlockSpec(memory_space=pltpu.VMEM)] * n


def exchange(v):
    blocks = v.reshape(16, v.shape[0] // 16, 128)
    return lax.all_to_all(blocks, "tm", 0, 0, tiled=True).reshape(v.shape)


def hbm(n):
    return [pl.BlockSpec(memory_space=pltpu.HBM)] * n


def call(kernel, outs, in_specs, scratch, us, mib, out_specs=None, aliases={}):
    more = {} if out_specs is None else {"out_specs": tuple(out_specs)}
    return pl.pallas_call(
        kernel,
        **more,
        input_output_aliases=aliases,
        out_shape=outs,
        in_specs=in_specs,
        scratch_shapes=scratch,
        compiler_params=pltpu.CompilerParams(vmem_limit_bytes=mib * MIB),
        cost_estimate=pl.CostEstimate(
            flops=int(us * 1.0e9), bytes_accessed=int(us * 3.0e6), transcendentals=0
        ),
    )


def across(axis, v, bit):
    return lax.ppermute(v, axis, [(s, s ^ bit) for s in range(16)])


def in_hbm(*arrays):
    return [pltpu.with_memory_space_constraint(v, pltpu.HBM) for v in arrays]


def pass_kernel(v_in, token, v_out):
    del v_in, token, v_out


def after(v, token):
    return pl.pallas_call(
        pass_kernel,
        out_shape=pltpu.HBM(v.shape, v.dtype),
        in_specs=hbm(2),
        out_specs=hbm(1)[0],
        input_output_aliases={0: 0},
    )(*in_hbm(v, token))


def weight_part(w_out):
    clip = lax.axis_index("clip")
    mine = lax.dynamic_slice(
        w_out.reshape(2, 64, MODEL), (0, 16 * (clip // 4), 256 * lax.rem(clip, 4)), (2, 16, 256)
    )
    return lax.all_to_all(jnp.tile(mine, (8, 1, 1)), "tm", 0, 0, tiled=True)


def gather_weight(part):
    for step in range(2):
        got = [part]
        for bits in (1, 2, 3):
            to = []
            for device in range(256):
                along_x = (device % 2) != step
                to.append((device, device ^ ((bits * 64) if along_x else (bits * 16))))
            got.append(lax.ppermute(part, ("clip", "tm"), to))
        part = jnp.stack(got)
    return part, across("tm", part, 1)


def on_device(x_inner, bc_inputs, step_raw, decay_rate, skip_gain, w_out, grad_out):
    x, bc, grad = x_inner[0], bc_inputs[0], grad_out[0]
    raw = step_raw[0].T
    gain = skip_gain.reshape(1, HEADS)
    tm, clip = lax.axis_index("tm"), lax.axis_index("clip")
    core = jnp.stack([lax.rem(tm, 2), clip // 4, lax.rem(clip, 4)]).astype(jnp.int32)
    along_z = [[2 * z + c for z in range(8)] for c in range(2)]
    wide = pltpu.VMEM((ROWS * SENT, 128), F32)

    part = weight_part(w_out)
    ahead = call(
        spatial_forward_kernel,
        shape(ROWS * SENT, 128),
        hbm(4) + vmem(1),
        [
            wide,
            pltpu.VMEM((ROWS, 2048), BF16),
            pltpu.VMEM((ROWS, 256), BF16),
            pltpu.VMEM((2 * HEADS, ROWS), BF16),
            pltpu.VMEM((ROWS, MODEL), BF16),
            pltpu.SemaphoreType.DMA((7,)),
        ],
        4,
        16,
    )(*in_hbm(x, bc, raw, grad), decay_rate)
    mine, theirs = gather_weight(after(part, ahead))
    ahead = exchange(ahead)

    kept = [(ROWS, 2048), (ROWS, 2048), (ROWS, MODEL), (ROWS, 128), (ROWS, 128), (8, 128, MODEL)]
    types = [BF16, BF16, BF16, BF16, F32, BF16]
    x_t, mixed, grad_t, bc_t, raw_t, other = call(
        temporal_forward_kernel,
        tuple(pltpu.HBM(dims, dtype) for dims, dtype in zip(kept, types)),
        [smem()] + vmem(2) + [smem()],
        [wide]
        + [pltpu.VMEM(dims, dtype) for dims, dtype in zip(kept, types)]
        + [pltpu.SemaphoreType.DMA((15,))],
        4,
        20,
        out_specs=hbm(6),
    )(core, ahead, decay_rate, gain)

    got = across("tm", other, 1)
    partial = call(
        weight_grad_kernel,
        (pltpu.HBM((8, 128, MODEL), BF16),),
        [smem()] + hbm(2) + vmem(1),
        [
            pltpu.VMEM((ROWS, 2048), BF16),
            pltpu.VMEM((ROWS, MODEL), BF16),
            pltpu.VMEM((8, 128, MODEL), BF16),
            pltpu.SemaphoreType.DMA((6,)),
        ],
        3,
        14,
        out_specs=hbm(1),
    )(core, *in_hbm(mixed, grad_t), got)[0]
    grad_w = lax.psum_scatter(
        partial, "tm", scatter_dimension=0, axis_index_groups=along_z, tiled=False
    )
    raw_t = after(raw_t, partial)

    back = call(
        temporal_backward_kernel,
        shape(ROWS * SENT, 128),
        [smem()] + hbm(7) + vmem(1) + [smem()],
        [wide, pltpu.VMEM((16, 2, 4, 16, MODEL), BF16), pltpu.VMEM((ROWS, 2048), BF16)]
        + [pltpu.VMEM(dims, dtype) for dims, dtype in zip(kept[:5], types)]
        + scan_scratch()
        + [pltpu.SemaphoreType.DMA((37,))],
        7,
        24,
    )(core, *in_hbm(x_t, mixed, grad_t, bc_t, raw_t, mine, theirs), decay_rate, gain)
    back = exchange(back)

    mixed_out, grad_x, grad_bc, grad_step = call(
        spatial_backward_kernel,
        (shape(ROWS, MODEL), shape(ROWS, 2048), shape(ROWS, 256), shape(2 * HEADS, ROWS)),
        vmem(5),
        [wide] + scan_scratch()[:2] + [pltpu.VMEM((ROWS, 2048), F32)],
        8,
        18,
    )(x, back, bc, raw, decay_rate)
    return (mixed_out[None], grad_x[None], grad_bc[None], grad_step.T[None], grad_w.astype(F32))


def solution(mesh):
    rows = P(("clip", "tm"), None, None)
    return jax.shard_map(
        on_device,
        mesh=mesh,
        in_specs=(rows, rows, rows, P(), P(), P("tm", None), rows),
        out_specs=(rows, rows, rows, rows, P(("clip", "tm"), None)),
        check_vma=False,
    )
```

```python
import jax
import jax.numpy as jnp
from jax import lax
from jax.experimental import pallas as pl
from jax.experimental.pallas import tpu as pltpu
from jax.sharding import PartitionSpec as P

F32 = jnp.float32
BF16 = jnp.bfloat16
LOG2E = 1.4426950408889634
CAP = 8.0

ROWS = 192
HEADS = 32
PAIRS = 16
MODEL = 1024
FRAMES = 16
PATCHES = 12
TILES = MODEL // 128
SENT = PAIRS + TILES + 2
HIGH = lax.Precision.HIGHEST
MIB = 1024 * 1024

SPATIAL_FWD = (((0, 128), (0, 128)), ((128, 192), (0, 192)))
SPATIAL_BWD = (((0, 128), (0, 192)), ((128, 192), (128, 192)))
TEMPORAL = (((0, 128), (0, 128)), ((128, 192), (128, 192)))


def dot(a, b, contract=((1,), (0,)), precision=None):
    return lax.dot_general(
        a, b, (contract, ((), ())), precision=precision, preferred_element_type=F32
    )


def mask_of(temporal, transposed=False):
    i = lax.broadcasted_iota(jnp.int32, (ROWS, ROWS), 1 if transposed else 0)
    j = lax.broadcasted_iota(jnp.int32, (ROWS, ROWS), 0 if transposed else 1)
    keep = i >= j
    if temporal:
        keep = keep & ((i >> 4) == (j >> 4))
    return keep


def softplus(v):
    return jnp.maximum(v, 0.0) + jnp.log1p(jnp.exp(-jnp.abs(v)))


def decay_terms(raw, rate, temporal):
    step = softplus(raw)
    cum = dot(mask_of(temporal).astype(F32), step * rate, precision=HIGH) * (-LOG2E)
    return step, cum, jnp.log(step) * LOG2E - cum


def head_lanes(shape):
    return lax.broadcasted_iota(jnp.int32, shape, 1) < 64


def split_pair(v):
    low = head_lanes(v.shape)
    zero = jnp.zeros_like(v)
    return jnp.where(low, v, zero), jnp.where(low, zero, v)


def both_heads(pair, one_head):
    return jnp.concatenate([one_head(2 * pair), one_head(2 * pair + 1)], axis=0)


def pick_heads(v):
    return jnp.where(head_lanes((ROWS, 128)), v[:ROWS], v[ROWS:])


def padded(parts, block, lanes):
    out = []
    for v, (_, (c0, c1)) in zip(parts, block):
        row = [jnp.zeros((v.shape[0], c0), v.dtype)] if c0 else []
        row.append(v)
        if c1 < lanes:
            row.append(jnp.zeros((v.shape[0], lanes - c1), v.dtype))
        out.append(jnp.concatenate(row, axis=1) if len(row) > 1 else v)
    return jnp.concatenate(out, axis=0)


def scan_forward(blocks, gram, cum, from_row, x_pair, pair):
    def weights(h):
        parts = []
        for (i0, i1), (j0, j1) in blocks:
            e = jnp.exp2(jnp.minimum(cum[i0:i1, h : h + 1] + from_row[h : h + 1, j0:j1], CAP))
            parts.append((e * gram[i0:i1, j0:j1]).astype(BF16))
        return padded(parts, blocks, ROWS)

    return pick_heads(dot(both_heads(pair, weights), x_pair))


def scan_backward(
    blocks, gram_t, cum_row, from_col, x_pair, dy_pair, pair, dgram, rowsum, colsum=None, by_x=None
):
    products = dot(jnp.concatenate(split_pair(x_pair), axis=0), dy_pair, ((1,), (1,)))
    added = [None] * len(blocks)

    def weights(h):
        parts = []
        sums = []
        for n, ((j0, j1), (i0, i1)) in enumerate(blocks):
            e = jnp.exp2(jnp.minimum(from_col[j0:j1, h : h + 1] + cum_row[h : h + 1, i0:i1], CAP))
            w = e * gram_t[j0:j1, i0:i1]
            rounded = w.astype(BF16)
            if colsum is None:
                w = rounded.astype(F32)
            base = ROWS * (h - 2 * pair)
            p = products[base + j0 : base + j1, i0:i1]
            t = p * e
            added[n] = t if added[n] is None else added[n] + t
            m = p * w
            if colsum is not None:
                colsum[j0:j1, h : h + 1] = jnp.sum(m, axis=1, keepdims=True)
            sums.append((i0, i1, jnp.sum(m, axis=0, keepdims=True)))
            parts.append(rounded)
        (a0, a1, first), (b0, b1, second) = sums
        if b0 < a1:
            rowsum[h : h + 1, a0:b0] = first[:, : b0 - a0]
            rowsum[h : h + 1, b0:b1] = first[:, b0 - a0 :] + second
        else:
            rowsum[h : h + 1, a0:a1] = first
            rowsum[h : h + 1, b0:b1] = second
        return padded(parts, blocks, ROWS)

    dx = pick_heads(dot(both_heads(pair, weights), dy_pair))
    if colsum is None:
        by_x[:, 128 * pair : 128 * pair + 128] = dx * x_pair.astype(F32)
    for ((j0, j1), (i0, i1)), t in zip(blocks, added):
        dgram[j0:j1, i0:i1] += t
    return dx


def head_sums(v):
    lane = lax.broadcasted_iota(jnp.int32, (2048, 128), 0)
    head = lax.broadcasted_iota(jnp.int32, (2048, 128), 1)
    ones = ((lane >> 6) == head).astype(BF16)
    high = v.astype(BF16)
    rest = (v - high.astype(F32)).astype(BF16)
    both = dot(jnp.concatenate([high, rest], axis=0), ones)
    return (both[:ROWS] + both[ROWS:])[:, :HEADS]


def finish_backward(temporal, dgram, rowsum, col, b, c, raw, step, rate):
    dg = jnp.where(mask_of(temporal, True), dgram[...], 0.0).astype(BF16)
    db = dot(dg, c)
    dc = dot(dg, b, ((0,), (0,)))
    dcum = rowsum[...].T - col
    dlog = dot(mask_of(temporal, True).astype(F32), dcum, precision=HIGH)
    dstep = col / step - rate * dlog
    draw = dstep / (1.0 + jnp.exp(-raw))
    return jnp.concatenate([db, dc], axis=1), draw


def put_spatial(wide, row, v):
    wide[pl.ds(row, ROWS, stride=SENT), :] = v


def get_spatial(wide, row):
    return wide[pl.ds(row, ROWS, stride=SENT), :]


def put_temporal(wide, row, v):
    for p in range(PATCHES):
        wide[pl.ds(p * SENT + row, FRAMES, stride=PATCHES * SENT), :] = v[16 * p : 16 * p + 16]


def get_temporal(wide, row):
    return jnp.concatenate(
        [wide[pl.ds(p * SENT + row, FRAMES, stride=PATCHES * SENT), :] for p in range(PATCHES)], axis=0
    )


def spatial_forward_kernel(
    x_hbm, bc_hbm, raw_hbm, grad_hbm, rate_ref, out_ref, wide, x_ref, bc_ref, raw_ref, grad_ref, sems
):
    def load(n, src, dst):
        copy = pltpu.make_async_copy(src, dst, sems.at[n])
        copy.start()
        return copy

    maps = load(0, bc_hbm, bc_ref)
    steps = load(1, raw_hbm, raw_ref)
    quarters = [pl.ds(512 * q, 512) for q in range(4)]
    xs = [load(2 + q, x_hbm.at[:, quarters[q]], x_ref.at[:, quarters[q]]) for q in range(4)]
    grads = load(6, grad_hbm, grad_ref)
    steps.wait()
    raw = raw_ref[...].astype(F32).T
    put_spatial(wide, PAIRS + TILES + 1, jnp.concatenate([raw, jnp.zeros_like(raw)], axis=1))
    _, cum, from_col = decay_terms(raw[:, :HEADS], rate_ref[0:1, :], False)
    from_row = from_col.T
    maps.wait()
    put_spatial(wide, PAIRS + TILES, bc_ref[:, 128:].astype(F32))
    gram = dot(bc_ref[:, 64:128], bc_ref[:, 0:64], ((1,), (1,)))
    gram = jnp.where(mask_of(False), gram, 0.0)
    for g in range(PAIRS):
        if g % 4 == 0:
            xs[g // 4].wait()
        y = scan_forward(SPATIAL_FWD, gram, cum, from_row, x_ref[:, 128 * g : 128 * g + 128], g)
        put_spatial(wide, g, y)
    grads.wait()
    for k in range(TILES):
        put_spatial(wide, PAIRS + k, grad_ref[:, 128 * k : 128 * k + 128].astype(F32))
    out_ref[...] = wide[...].astype(BF16)


def weight_grad(mixed_ref, grad_ref, parity, column):
    lanes = [pl.ds(pl.multiple_of((2 * z + parity) * 128, 128), 128) for z in range(PAIRS // 2)]
    rows = jnp.concatenate([mixed_ref[:, at] for at in lanes], axis=1)
    return dot(rows, grad_ref[:, column : column + 256], ((0,), (0,)))


def temporal_forward_kernel(
    core_ref, here_ref, rate_ref, gain_ref,
    x_out, mixed_out, grad_out, bc_out, raw_out, other_out,
    wide, x_ref, mixed_ref, grad_ref, bc_ref, raw_ref, other_ref, sems,
):
    saves = []

    def save(src, dst):
        copy = pltpu.make_async_copy(src, dst, sems.at[len(saves)])
        copy.start()
        saves.append(copy)

    wide[...] = here_ref[...].astype(F32)
    for k in range(TILES):
        grad_ref[:, 128 * k : 128 * k + 128] = get_temporal(wide, PAIRS + k).astype(BF16)
    save(grad_ref, grad_out)
    bc = get_temporal(wide, PAIRS + TILES).astype(BF16)
    bc_ref[...] = bc
    save(bc_ref, bc_out)
    raw = get_temporal(wide, PAIRS + TILES + 1)
    raw_ref[...] = raw
    save(raw_ref, raw_out)
    _, cum, from_col = decay_terms(raw[:, HEADS : 2 * HEADS], rate_ref[1:2, :], True)
    from_row = from_col.T
    gram = dot(bc[:, 64:128], bc[:, 0:64], ((1,), (1,)))
    gram = jnp.where(mask_of(True), gram, 0.0)
    low = head_lanes((1, 128))
    for g in range(PAIRS):
        x = get_temporal(wide, g)
        xb = x.astype(BF16)
        x_ref[:, 128 * g : 128 * g + 128] = xb
        y = scan_forward(TEMPORAL, gram, cum, from_row, xb, g)
        gain = jnp.where(low, gain_ref[0, 2 * g], gain_ref[0, 2 * g + 1])
        mixed_ref[:, 128 * g : 128 * g + 128] = (y + gain * x).astype(BF16)
        if g % 4 == 3:
            at = pl.ds(128 * (g - 3), 512)
            save(x_ref.at[:, at], x_out.at[:, at])
            save(mixed_ref.at[:, at], mixed_out.at[:, at])
    for column in range(0, MODEL, 256):
        dw = weight_grad(mixed_ref, grad_ref, 1 - core_ref[0], column)
        at = pl.ds(column, 256)
        other_ref[:, :, at] = dw.reshape(8, 128, 256).astype(BF16)
        save(other_ref.at[:, :, at], other_out.at[:, :, at])
    for copy in saves:
        copy.wait()


def weight_grad_kernel(
    core_ref, mixed_ref, grad_ref, got_ref, out_hbm, out_ref, sems
):
    saves = []
    for n in range(MODEL // 256):
        at = pl.ds(256 * n, 256)
        dw = weight_grad(mixed_ref, grad_ref, core_ref[0], 256 * n).reshape(8, 128, 256)
        out_ref[:, :, at] = (dw + got_ref[:, :, at].astype(F32)).astype(BF16)
        saves.append(pltpu.make_async_copy(out_ref.at[:, :, at], out_hbm.at[:, :, at], sems.at[n]))
        saves[-1].start()
    for copy in saves:
        copy.wait()


def temporal_backward_kernel(
    place_ref, x_hbm, mixed_hbm, grad_hbm, bc_hbm, raw_hbm, mine_hbm, theirs_hbm, rate_ref, gain_ref,
    out_ref, wide, weight, dy_all, x_ref, mixed_ref, grad_ref, bc_ref, raw_ref,
    dgram, rowsum, colsum, sems,
):
    core, x, y = place_ref[0], place_ref[1], place_ref[2]
    pairs = [
        (raw_hbm, raw_ref),
        (bc_hbm, bc_ref),
        (grad_hbm, grad_ref),
        (x_hbm, x_ref),
        (mixed_hbm, mixed_ref),
    ]
    for src, half in ((mine_hbm, core), (theirs_hbm, 1 - core)):
        for a in range(4):
            for b in range(4):
                from_x = x ^ (a + half * (b - a))
                from_y = y ^ (b + half * (a - b))
                at = pl.ds(pl.multiple_of(256 * from_y, 256), 256)
                pairs.append((src.at[a, b], weight.at[:, half, from_x, :, at]))
    loads = [pltpu.make_async_copy(src, dst, sems.at[n]) for n, (src, dst) in enumerate(pairs)]
    for copy in loads:
        copy.start()
    loads[0].wait()
    raw = raw_ref[:, HEADS : 2 * HEADS]
    rate = rate_ref[1:2, :]
    step, cum, from_col = decay_terms(raw, rate, True)
    cum_row = cum.T
    loads[1].wait()
    b, c = bc_ref[:, 0:64], bc_ref[:, 64:128]
    gram_t = jnp.where(mask_of(True, True), dot(b, c, ((1,), (1,))), 0.0)
    dgram[...] = jnp.zeros_like(dgram)
    low = head_lanes((1, 128))
    for copy in loads[2:]:
        copy.wait()
    for z in range(PAIRS // 2):
        w = weight[2 * z : 2 * z + 2].reshape(256, MODEL)
        dy_all[:, 256 * z : 256 * z + 256] = dot(grad_ref[...], w, ((1,), (1,))).astype(BF16)
    for g in range(PAIRS):
        dy = dy_all[:, 128 * g : 128 * g + 128]
        dx = scan_backward(
            TEMPORAL, gram_t, cum_row, from_col, x_ref[:, 128 * g : 128 * g + 128], dy, g,
            dgram, rowsum, colsum,
        )
        gain = jnp.where(low, gain_ref[0, 2 * g], gain_ref[0, 2 * g + 1])
        put_temporal(wide, g, dx + gain * dy.astype(F32))
    dbc, draw = finish_backward(True, dgram, rowsum, colsum[...], b, c, raw, step, rate)
    put_temporal(wide, PAIRS + TILES, dbc)
    put_temporal(
        wide, PAIRS + TILES + 1, jnp.concatenate([draw, jnp.zeros((ROWS, 128 - HEADS), F32)], axis=1)
    )
    for k in range(0, TILES, 2):
        w = weight[:, :, :, :, 128 * k : 128 * k + 256].reshape(2048, 256)
        projected = dot(mixed_ref[...], w)
        for t in range(2):
            put_temporal(wide, PAIRS + k + t, projected[:, 128 * t : 128 * t + 128])
    out_ref[...] = wide[...].astype(BF16)


def spatial_backward_kernel(
    x_ref, back_ref, bc_ref, raw_ref, rate_ref, out_ref, dx_ref, dbc_ref, draw_ref,
    wide, dgram, rowsum, by_x,
):
    wide[...] = back_ref[...].astype(F32)
    for k in range(TILES):
        out_ref[:, 128 * k : 128 * k + 128] = get_spatial(wide, PAIRS + k).astype(BF16)
    raw = raw_ref[...].astype(F32).T[:, :HEADS]
    rate = rate_ref[0:1, :]
    step, cum, from_col = decay_terms(raw, rate, False)
    cum_row = cum.T
    b, c = bc_ref[:, 0:64], bc_ref[:, 64:128]
    gram_t = jnp.where(mask_of(False, True), dot(b, c, ((1,), (1,))), 0.0)
    dgram[...] = jnp.zeros_like(dgram)
    for g in range(PAIRS):
        dy = get_spatial(wide, g).astype(BF16)
        dx = scan_backward(
            SPATIAL_BWD, gram_t, cum_row, from_col, x_ref[:, 128 * g : 128 * g + 128], dy, g,
            dgram, rowsum, by_x=by_x,
        )
        dx_ref[:, 128 * g : 128 * g + 128] = dx.astype(BF16)
    dbc, draw = finish_backward(False, dgram, rowsum, head_sums(by_x[...]), b, c, raw, step, rate)
    dbc_ref[:, 0:128] = dbc.astype(BF16)
    dbc_ref[:, 128:256] = get_spatial(wide, PAIRS + TILES).astype(BF16)
    draw_t = get_spatial(wide, PAIRS + TILES + 1)
    draw_ref[...] = jnp.concatenate([draw, draw_t[:, :HEADS]], axis=1).T.astype(BF16)


def shape(*dims, dtype=BF16):
    return jax.ShapeDtypeStruct(dims, dtype)


def scan_scratch():
    return [
        pltpu.VMEM((ROWS, ROWS), F32),
        pltpu.VMEM((HEADS, ROWS), F32),
        pltpu.VMEM((ROWS, HEADS), F32),
    ]


def smem():
    return pl.BlockSpec(memory_space=pltpu.SMEM)


def vmem(n):
    return [pl.BlockSpec(memory_space=pltpu.VMEM)] * n


def exchange(v):
    blocks = v.reshape(16, v.shape[0] // 16, 128)
    return lax.all_to_all(blocks, "tm", 0, 0, tiled=True).reshape(v.shape)


def hbm(n):
    return [pl.BlockSpec(memory_space=pltpu.HBM)] * n


def call(kernel, outs, in_specs, scratch, us, mib, out_specs=None, aliases={}):
    more = {} if out_specs is None else {"out_specs": tuple(out_specs)}
    return pl.pallas_call(
        kernel,
        **more,
        input_output_aliases=aliases,
        out_shape=outs,
        in_specs=in_specs,
        scratch_shapes=scratch,
        compiler_params=pltpu.CompilerParams(vmem_limit_bytes=mib * MIB),
        cost_estimate=pl.CostEstimate(
            flops=int(us * 1.0e9), bytes_accessed=int(us * 3.0e6), transcendentals=0
        ),
    )


def across(axis, v, bit):
    return lax.ppermute(v, axis, [(s, s ^ bit) for s in range(16)])


def in_hbm(*arrays):
    return [pltpu.with_memory_space_constraint(v, pltpu.HBM) for v in arrays]


def pass_kernel(v_in, token, v_out):
    del v_in, token, v_out


def after(v, token):
    return pl.pallas_call(
        pass_kernel,
        out_shape=pltpu.HBM(v.shape, v.dtype),
        in_specs=hbm(2),
        out_specs=hbm(1)[0],
        input_output_aliases={0: 0},
    )(*in_hbm(v, token))


def weight_part(w_out):
    clip = lax.axis_index("clip")
    mine = lax.dynamic_slice(
        w_out.reshape(2, 64, MODEL), (0, 16 * (clip // 4), 256 * lax.rem(clip, 4)), (2, 16, 256)
    )
    return lax.all_to_all(jnp.tile(mine, (8, 1, 1)), "tm", 0, 0, tiled=True)


def gather_weight(part):
    for step in range(2):
        got = [part]
        for bits in (1, 2, 3):
            to = []
            for device in range(256):
                along_x = (device % 2) != step
                to.append((device, device ^ ((bits * 64) if along_x else (bits * 16))))
            got.append(lax.ppermute(part, ("clip", "tm"), to))
        part = jnp.stack(got)
    return part, across("tm", part, 1)


def on_device(x_inner, bc_inputs, step_raw, decay_rate, skip_gain, w_out, grad_out):
    x, bc, grad = x_inner[0], bc_inputs[0], grad_out[0]
    raw = step_raw[0].T
    gain = skip_gain.reshape(1, HEADS)
    tm, clip = lax.axis_index("tm"), lax.axis_index("clip")
    core = jnp.stack([lax.rem(tm, 2), clip // 4, lax.rem(clip, 4)]).astype(jnp.int32)
    along_z = [[2 * z + c for z in range(8)] for c in range(2)]
    wide = pltpu.VMEM((ROWS * SENT, 128), F32)

    part = weight_part(w_out)
    ahead = call(
        spatial_forward_kernel,
        shape(ROWS * SENT, 128),
        hbm(4) + vmem(1),
        [
            wide,
            pltpu.VMEM((ROWS, 2048), BF16),
            pltpu.VMEM((ROWS, 256), BF16),
            pltpu.VMEM((2 * HEADS, ROWS), BF16),
            pltpu.VMEM((ROWS, MODEL), BF16),
            pltpu.SemaphoreType.DMA((7,)),
        ],
        4,
        16,
    )(*in_hbm(x, bc, raw, grad), decay_rate)
    mine, theirs = gather_weight(after(part, ahead))
    ahead = exchange(ahead)

    kept = [(ROWS, 2048), (ROWS, 2048), (ROWS, MODEL), (ROWS, 128), (ROWS, 128), (8, 128, MODEL)]
    types = [BF16, BF16, BF16, BF16, F32, BF16]
    x_t, mixed, grad_t, bc_t, raw_t, other = call(
        temporal_forward_kernel,
        tuple(pltpu.HBM(dims, dtype) for dims, dtype in zip(kept, types)),
        [smem()] + vmem(2) + [smem()],
        [wide]
        + [pltpu.VMEM(dims, dtype) for dims, dtype in zip(kept, types)]
        + [pltpu.SemaphoreType.DMA((15,))],
        4,
        20,
        out_specs=hbm(6),
    )(core, ahead, decay_rate, gain)

    got = across("tm", other, 1)
    partial = call(
        weight_grad_kernel,
        (pltpu.HBM((8, 128, MODEL), BF16),),
        [smem()] + vmem(3),
        [pltpu.VMEM((8, 128, MODEL), BF16), pltpu.SemaphoreType.DMA((4,))],
        3,
        14,
        out_specs=hbm(1),
    )(core, mixed, grad_t, got)[0]
    grad_w = lax.psum_scatter(
        partial, "tm", scatter_dimension=0, axis_index_groups=along_z, tiled=False
    )
    raw_t = after(raw_t, partial)

    back = call(
        temporal_backward_kernel,
        shape(ROWS * SENT, 128),
        [smem()] + hbm(6) + [pl.BlockSpec(memory_space=pl.ANY)] + vmem(1) + [smem()],
        [wide, pltpu.VMEM((16, 2, 4, 16, MODEL), BF16), pltpu.VMEM((ROWS, 2048), BF16)]
        + [pltpu.VMEM(dims, dtype) for dims, dtype in zip(kept[:5], types)]
        + scan_scratch()
        + [pltpu.SemaphoreType.DMA((37,))],
        7,
        24,
    )(core, *in_hbm(x_t, mixed, grad_t, bc_t, raw_t, mine), theirs, decay_rate, gain)
    back = exchange(back)

    mixed_out, grad_x, grad_bc, grad_step = call(
        spatial_backward_kernel,
        (shape(ROWS, MODEL), shape(ROWS, 2048), shape(ROWS, 256), shape(2 * HEADS, ROWS)),
        vmem(5),
        [wide] + scan_scratch()[:2] + [pltpu.VMEM((ROWS, 2048), F32)],
        8,
        18,
    )(x, back, bc, raw, decay_rate)
    return (mixed_out[None], grad_x[None], grad_bc[None], grad_step.T[None], grad_w.astype(F32))


def solution(mesh):
    rows = P(("clip", "tm"), None, None)
    return jax.shard_map(
        on_device,
        mesh=mesh,
        in_specs=(rows, rows, rows, P(), P(), P("tm", None), rows),
        out_specs=(rows, rows, rows, rows, P(("clip", "tm"), None)),
        check_vma=False,
    )
```

```python
import jax
import jax.numpy as jnp
from jax import lax
from jax.experimental import pallas as pl
from jax.experimental.pallas import tpu as pltpu
from jax.sharding import PartitionSpec as P

F32 = jnp.float32
BF16 = jnp.bfloat16
LOG2E = 1.4426950408889634
CAP = 8.0

ROWS = 192
HEADS = 32
PAIRS = 16
MODEL = 1024
FRAMES = 16
PATCHES = 12
TILES = MODEL // 128
SENT = PAIRS + TILES + 2
HIGH = lax.Precision.HIGHEST
MIB = 1024 * 1024

SPATIAL_FWD = (((0, 128), (0, 128)), ((128, 192), (0, 192)))
SPATIAL_BWD = (((0, 128), (0, 192)), ((128, 192), (128, 192)))
TEMPORAL = (((0, 128), (0, 128)), ((128, 192), (128, 192)))


def dot(a, b, contract=((1,), (0,)), precision=None):
    return lax.dot_general(
        a, b, (contract, ((), ())), precision=precision, preferred_element_type=F32
    )


def mask_of(temporal, transposed=False):
    i = lax.broadcasted_iota(jnp.int32, (ROWS, ROWS), 1 if transposed else 0)
    j = lax.broadcasted_iota(jnp.int32, (ROWS, ROWS), 0 if transposed else 1)
    keep = i >= j
    if temporal:
        keep = keep & ((i >> 4) == (j >> 4))
    return keep


def softplus(v):
    return jnp.maximum(v, 0.0) + jnp.log1p(jnp.exp(-jnp.abs(v)))


def decay_terms(raw, rate, temporal):
    step = softplus(raw)
    cum = dot(mask_of(temporal).astype(F32), step * rate, precision=HIGH) * (-LOG2E)
    return step, cum, jnp.log(step) * LOG2E - cum


def head_lanes(shape):
    return lax.broadcasted_iota(jnp.int32, shape, 1) < 64


def split_pair(v):
    low = head_lanes(v.shape)
    zero = jnp.zeros_like(v)
    return jnp.where(low, v, zero), jnp.where(low, zero, v)


def both_heads(pair, one_head):
    return jnp.concatenate([one_head(2 * pair), one_head(2 * pair + 1)], axis=0)


def pick_heads(v):
    return jnp.where(head_lanes((ROWS, 128)), v[:ROWS], v[ROWS:])


def padded(parts, block, lanes):
    out = []
    for v, (_, (c0, c1)) in zip(parts, block):
        row = [jnp.zeros((v.shape[0], c0), v.dtype)] if c0 else []
        row.append(v)
        if c1 < lanes:
            row.append(jnp.zeros((v.shape[0], lanes - c1), v.dtype))
        out.append(jnp.concatenate(row, axis=1) if len(row) > 1 else v)
    return jnp.concatenate(out, axis=0)


def scan_forward(blocks, gram, cum, from_row, x_pair, pair):
    def weights(h):
        parts = []
        for (i0, i1), (j0, j1) in blocks:
            e = jnp.exp2(jnp.minimum(cum[i0:i1, h : h + 1] + from_row[h : h + 1, j0:j1], CAP))
            parts.append((e * gram[i0:i1, j0:j1]).astype(BF16))
        return padded(parts, blocks, ROWS)

    return pick_heads(dot(both_heads(pair, weights), x_pair))


def scan_backward(
    blocks, gram_t, cum_row, from_col, x_pair, dy_pair, pair, dgram, rowsum, colsum=None, by_x=None
):
    products = dot(jnp.concatenate(split_pair(x_pair), axis=0), dy_pair, ((1,), (1,)))
    added = [None] * len(blocks)

    def weights(h):
        parts = []
        sums = []
        for n, ((j0, j1), (i0, i1)) in enumerate(blocks):
            e = jnp.exp2(jnp.minimum(from_col[j0:j1, h : h + 1] + cum_row[h : h + 1, i0:i1], CAP))
            w = e * gram_t[j0:j1, i0:i1]
            rounded = w.astype(BF16)
            if colsum is None:
                w = rounded.astype(F32)
            base = ROWS * (h - 2 * pair)
            p = products[base + j0 : base + j1, i0:i1]
            t = p * e
            added[n] = t if added[n] is None else added[n] + t
            m = p * w
            if colsum is not None:
                colsum[j0:j1, h : h + 1] = jnp.sum(m, axis=1, keepdims=True)
            sums.append((i0, i1, jnp.sum(m, axis=0, keepdims=True)))
            parts.append(rounded)
        (a0, a1, first), (b0, b1, second) = sums
        if b0 < a1:
            rowsum[h : h + 1, a0:b0] = first[:, : b0 - a0]
            rowsum[h : h + 1, b0:b1] = first[:, b0 - a0 :] + second
        else:
            rowsum[h : h + 1, a0:a1] = first
            rowsum[h : h + 1, b0:b1] = second
        return padded(parts, blocks, ROWS)

    dx = pick_heads(dot(both_heads(pair, weights), dy_pair))
    if colsum is None:
        by_x[:, 128 * pair : 128 * pair + 128] = dx * x_pair.astype(F32)
    for ((j0, j1), (i0, i1)), t in zip(blocks, added):
        dgram[j0:j1, i0:i1] += t
    return dx


def head_sums(v):
    lane = lax.broadcasted_iota(jnp.int32, (2048, 128), 0)
    head = lax.broadcasted_iota(jnp.int32, (2048, 128), 1)
    ones = ((lane >> 6) == head).astype(BF16)
    high = v.astype(BF16)
    rest = (v - high.astype(F32)).astype(BF16)
    both = dot(jnp.concatenate([high, rest], axis=0), ones)
    return (both[:ROWS] + both[ROWS:])[:, :HEADS]


def finish_backward(temporal, dgram, rowsum, col, b, c, raw, step, rate):
    dg = jnp.where(mask_of(temporal, True), dgram[...], 0.0).astype(BF16)
    db = dot(dg, c)
    dc = dot(dg, b, ((0,), (0,)))
    dcum = rowsum[...].T - col
    dlog = dot(mask_of(temporal, True).astype(F32), dcum, precision=HIGH)
    dstep = col / step - rate * dlog
    draw = dstep / (1.0 + jnp.exp(-raw))
    return jnp.concatenate([db, dc], axis=1), draw


def put_spatial(wide, row, v):
    wide[pl.ds(row, ROWS, stride=SENT), :] = v


def get_spatial(wide, row):
    return wide[pl.ds(row, ROWS, stride=SENT), :]


def put_temporal(wide, row, v):
    for p in range(PATCHES):
        wide[pl.ds(p * SENT + row, FRAMES, stride=PATCHES * SENT), :] = v[16 * p : 16 * p + 16]


def get_temporal(wide, row):
    return jnp.concatenate(
        [wide[pl.ds(p * SENT + row, FRAMES, stride=PATCHES * SENT), :] for p in range(PATCHES)], axis=0
    )


def spatial_forward_kernel(
    x_hbm, bc_hbm, raw_hbm, grad_hbm, rate_ref, out_ref, wide, x_ref, bc_ref, raw_ref, grad_ref, sems
):
    def load(n, src, dst):
        copy = pltpu.make_async_copy(src, dst, sems.at[n])
        copy.start()
        return copy

    maps = load(0, bc_hbm, bc_ref)
    steps = load(1, raw_hbm, raw_ref)
    quarters = [pl.ds(512 * q, 512) for q in range(4)]
    xs = [load(2 + q, x_hbm.at[:, quarters[q]], x_ref.at[:, quarters[q]]) for q in range(4)]
    grads = load(6, grad_hbm, grad_ref)
    steps.wait()
    raw = raw_ref[...].astype(F32).T
    put_spatial(wide, PAIRS + TILES + 1, jnp.concatenate([raw, jnp.zeros_like(raw)], axis=1))
    _, cum, from_col = decay_terms(raw[:, :HEADS], rate_ref[0:1, :], False)
    from_row = from_col.T
    maps.wait()
    put_spatial(wide, PAIRS + TILES, bc_ref[:, 128:].astype(F32))
    gram = dot(bc_ref[:, 64:128], bc_ref[:, 0:64], ((1,), (1,)))
    gram = jnp.where(mask_of(False), gram, 0.0)
    for g in range(PAIRS):
        if g % 4 == 0:
            xs[g // 4].wait()
        y = scan_forward(SPATIAL_FWD, gram, cum, from_row, x_ref[:, 128 * g : 128 * g + 128], g)
        put_spatial(wide, g, y)
    grads.wait()
    for k in range(TILES):
        put_spatial(wide, PAIRS + k, grad_ref[:, 128 * k : 128 * k + 128].astype(F32))
    out_ref[...] = wide[...].astype(BF16)


def weight_grad(mixed_ref, grad_ref, parity, column):
    lanes = [pl.ds(pl.multiple_of((2 * z + parity) * 128, 128), 128) for z in range(PAIRS // 2)]
    rows = jnp.concatenate([mixed_ref[:, at] for at in lanes], axis=1)
    return dot(rows, grad_ref[:, column : column + 256], ((0,), (0,)))


def temporal_forward_kernel(
    core_ref, here_ref, rate_ref, gain_ref,
    x_out, mixed_out, grad_out, bc_out, raw_out, other_out,
    wide, x_ref, mixed_ref, grad_ref, bc_ref, raw_ref, other_ref, sems,
):
    saves = []

    def save(src, dst):
        copy = pltpu.make_async_copy(src, dst, sems.at[len(saves)])
        copy.start()
        saves.append(copy)

    wide[...] = here_ref[...].astype(F32)
    for k in range(TILES):
        grad_ref[:, 128 * k : 128 * k + 128] = get_temporal(wide, PAIRS + k).astype(BF16)
    save(grad_ref, grad_out)
    bc = get_temporal(wide, PAIRS + TILES).astype(BF16)
    bc_ref[...] = bc
    save(bc_ref, bc_out)
    raw = get_temporal(wide, PAIRS + TILES + 1)
    raw_ref[...] = raw
    save(raw_ref, raw_out)
    _, cum, from_col = decay_terms(raw[:, HEADS : 2 * HEADS], rate_ref[1:2, :], True)
    from_row = from_col.T
    gram = dot(bc[:, 64:128], bc[:, 0:64], ((1,), (1,)))
    gram = jnp.where(mask_of(True), gram, 0.0)
    low = head_lanes((1, 128))
    for g in range(PAIRS):
        x = get_temporal(wide, g)
        xb = x.astype(BF16)
        x_ref[:, 128 * g : 128 * g + 128] = xb
        y = scan_forward(TEMPORAL, gram, cum, from_row, xb, g)
        gain = jnp.where(low, gain_ref[0, 2 * g], gain_ref[0, 2 * g + 1])
        mixed_ref[:, 128 * g : 128 * g + 128] = (y + gain * x).astype(BF16)
        if g % 4 == 3:
            at = pl.ds(128 * (g - 3), 512)
            save(x_ref.at[:, at], x_out.at[:, at])
            save(mixed_ref.at[:, at], mixed_out.at[:, at])
    for column in range(0, MODEL, 256):
        dw = weight_grad(mixed_ref, grad_ref, 1 - core_ref[0], column)
        at = pl.ds(column, 256)
        other_ref[:, :, at] = dw.reshape(8, 128, 256).astype(BF16)
        save(other_ref.at[:, :, at], other_out.at[:, :, at])
    for copy in saves:
        copy.wait()


def weight_grad_kernel(
    core_ref, mixed_ref, grad_ref, got_ref, out_hbm, out_ref, sems
):
    saves = []
    for n in range(MODEL // 256):
        at = pl.ds(256 * n, 256)
        dw = weight_grad(mixed_ref, grad_ref, core_ref[0], 256 * n).reshape(8, 128, 256)
        out_ref[:, :, at] = (dw + got_ref[:, :, at].astype(F32)).astype(BF16)
        saves.append(pltpu.make_async_copy(out_ref.at[:, :, at], out_hbm.at[:, :, at], sems.at[n]))
        saves[-1].start()
    for copy in saves:
        copy.wait()


def temporal_backward_kernel(
    place_ref, x_hbm, mixed_hbm, grad_hbm, bc_hbm, raw_hbm, mine_hbm, theirs_hbm, rate_ref, gain_ref,
    out_ref, wide, weight, dy_all, x_ref, mixed_ref, grad_ref, bc_ref, raw_ref,
    dgram, rowsum, colsum, sems,
):
    core, x, y = place_ref[0], place_ref[1], place_ref[2]
    pairs = [
        (raw_hbm, raw_ref),
        (bc_hbm, bc_ref),
        (grad_hbm, grad_ref),
        (x_hbm, x_ref),
        (mixed_hbm, mixed_ref),
    ]
    for src, half in ((mine_hbm, core), (theirs_hbm, 1 - core)):
        for a in range(4):
            for b in range(4):
                from_x = x ^ (a + half * (b - a))
                from_y = y ^ (b + half * (a - b))
                at = pl.ds(pl.multiple_of(256 * from_y, 256), 256)
                pairs.append((src.at[a, b], weight.at[:, half, from_x, :, at]))
    loads = [pltpu.make_async_copy(src, dst, sems.at[n]) for n, (src, dst) in enumerate(pairs)]
    for copy in loads:
        copy.start()
    loads[0].wait()
    raw = raw_ref[:, HEADS : 2 * HEADS]
    rate = rate_ref[1:2, :]
    step, cum, from_col = decay_terms(raw, rate, True)
    cum_row = cum.T
    loads[1].wait()
    b, c = bc_ref[:, 0:64], bc_ref[:, 64:128]
    gram_t = jnp.where(mask_of(True, True), dot(b, c, ((1,), (1,))), 0.0)
    dgram[...] = jnp.zeros_like(dgram)
    low = head_lanes((1, 128))
    for copy in loads[2:]:
        copy.wait()
    for z in range(PAIRS // 2):
        w = weight[2 * z : 2 * z + 2].reshape(256, MODEL)
        dy_all[:, 256 * z : 256 * z + 256] = dot(grad_ref[...], w, ((1,), (1,))).astype(BF16)
    for g in range(PAIRS):
        dy = dy_all[:, 128 * g : 128 * g + 128]
        dx = scan_backward(
            TEMPORAL, gram_t, cum_row, from_col, x_ref[:, 128 * g : 128 * g + 128], dy, g,
            dgram, rowsum, colsum,
        )
        gain = jnp.where(low, gain_ref[0, 2 * g], gain_ref[0, 2 * g + 1])
        put_temporal(wide, g, dx + gain * dy.astype(F32))
    dbc, draw = finish_backward(True, dgram, rowsum, colsum[...], b, c, raw, step, rate)
    put_temporal(wide, PAIRS + TILES, dbc)
    put_temporal(
        wide, PAIRS + TILES + 1, jnp.concatenate([draw, jnp.zeros((ROWS, 128 - HEADS), F32)], axis=1)
    )
    for k in range(0, TILES, 2):
        w = weight[:, :, :, :, 128 * k : 128 * k + 256].reshape(2048, 256)
        projected = dot(mixed_ref[...], w)
        for t in range(2):
            put_temporal(wide, PAIRS + k + t, projected[:, 128 * t : 128 * t + 128])
    out_ref[...] = wide[...].astype(BF16)


def spatial_backward_kernel(
    x_ref, back_ref, bc_ref, raw_ref, rate_ref, out_ref, dx_ref, dbc_ref, draw_ref,
    wide, dgram, rowsum, by_x,
):
    wide[...] = back_ref[...].astype(F32)
    for k in range(TILES):
        out_ref[:, 128 * k : 128 * k + 128] = get_spatial(wide, PAIRS + k).astype(BF16)
    raw = raw_ref[...].astype(F32).T[:, :HEADS]
    rate = rate_ref[0:1, :]
    step, cum, from_col = decay_terms(raw, rate, False)
    cum_row = cum.T
    b, c = bc_ref[:, 0:64], bc_ref[:, 64:128]
    gram_t = jnp.where(mask_of(False, True), dot(b, c, ((1,), (1,))), 0.0)
    dgram[...] = jnp.zeros_like(dgram)
    for g in range(PAIRS):
        dy = get_spatial(wide, g).astype(BF16)
        dx = scan_backward(
            SPATIAL_BWD, gram_t, cum_row, from_col, x_ref[:, 128 * g : 128 * g + 128], dy, g,
            dgram, rowsum, by_x=by_x,
        )
        dx_ref[:, 128 * g : 128 * g + 128] = dx.astype(BF16)
    dbc, draw = finish_backward(False, dgram, rowsum, head_sums(by_x[...]), b, c, raw, step, rate)
    dbc_ref[:, 0:128] = dbc.astype(BF16)
    dbc_ref[:, 128:256] = get_spatial(wide, PAIRS + TILES).astype(BF16)
    draw_t = get_spatial(wide, PAIRS + TILES + 1)
    draw_ref[...] = jnp.concatenate([draw, draw_t[:, :HEADS]], axis=1).T.astype(BF16)


def shape(*dims, dtype=BF16):
    return jax.ShapeDtypeStruct(dims, dtype)


def scan_scratch():
    return [
        pltpu.VMEM((ROWS, ROWS), F32),
        pltpu.VMEM((HEADS, ROWS), F32),
        pltpu.VMEM((ROWS, HEADS), F32),
    ]


def smem():
    return pl.BlockSpec(memory_space=pltpu.SMEM)


def vmem(n):
    return [pl.BlockSpec(memory_space=pltpu.VMEM)] * n


def exchange(v):
    blocks = v.reshape(16, v.shape[0] // 16, 128)
    return lax.all_to_all(blocks, "tm", 0, 0, tiled=True).reshape(v.shape)


def hbm(n):
    return [pl.BlockSpec(memory_space=pltpu.HBM)] * n


def call(kernel, outs, in_specs, scratch, us, mib, out_specs=None, aliases={}):
    more = {} if out_specs is None else {"out_specs": tuple(out_specs)}
    return pl.pallas_call(
        kernel,
        **more,
        input_output_aliases=aliases,
        out_shape=outs,
        in_specs=in_specs,
        scratch_shapes=scratch,
        compiler_params=pltpu.CompilerParams(vmem_limit_bytes=mib * MIB),
        cost_estimate=pl.CostEstimate(
            flops=int(us * 1.0e9), bytes_accessed=int(us * 3.0e6), transcendentals=0
        ),
    )


def across(axis, v, bit):
    return lax.ppermute(v, axis, [(s, s ^ bit) for s in range(16)])


def in_hbm(*arrays):
    return [pltpu.with_memory_space_constraint(v, pltpu.HBM) for v in arrays]


def pass_kernel(v_in, token, v_out):
    del v_in, token, v_out


def after(v, token):
    return pl.pallas_call(
        pass_kernel,
        out_shape=pltpu.HBM(v.shape, v.dtype),
        in_specs=hbm(2),
        out_specs=hbm(1)[0],
        input_output_aliases={0: 0},
    )(*in_hbm(v, token))


def weight_part(w_out):
    clip = lax.axis_index("clip")
    mine = lax.dynamic_slice(
        w_out.reshape(2, 64, MODEL), (0, 16 * (clip // 4), 256 * lax.rem(clip, 4)), (2, 16, 256)
    )
    return lax.all_to_all(jnp.tile(mine, (8, 1, 1)), "tm", 0, 0, tiled=True)


def gather_weight(part):
    for step in range(2):
        got = [part]
        for bits in (1, 2, 3):
            to = []
            for device in range(256):
                along_x = (device % 2) != step
                to.append((device, device ^ ((bits * 64) if along_x else (bits * 16))))
            got.append(lax.ppermute(part, ("clip", "tm"), to))
        part = jnp.stack(got)
    return part, across("tm", part, 1)


def on_device(x_inner, bc_inputs, step_raw, decay_rate, skip_gain, w_out, grad_out):
    x, bc, grad = x_inner[0], bc_inputs[0], grad_out[0]
    raw = step_raw[0].T
    gain = skip_gain.reshape(1, HEADS)
    tm, clip = lax.axis_index("tm"), lax.axis_index("clip")
    core = jnp.stack([lax.rem(tm, 2), clip // 4, lax.rem(clip, 4)]).astype(jnp.int32)
    along_z = [[2 * z + c for z in range(8)] for c in range(2)]
    wide = pltpu.VMEM((ROWS * SENT, 128), F32)

    part = weight_part(w_out)
    ahead = call(
        spatial_forward_kernel,
        shape(ROWS * SENT, 128),
        hbm(4) + vmem(1),
        [
            wide,
            pltpu.VMEM((ROWS, 2048), BF16),
            pltpu.VMEM((ROWS, 256), BF16),
            pltpu.VMEM((2 * HEADS, ROWS), BF16),
            pltpu.VMEM((ROWS, MODEL), BF16),
            pltpu.SemaphoreType.DMA((7,)),
        ],
        4,
        16,
    )(*in_hbm(x, bc, raw, grad), decay_rate)
    mine, theirs = gather_weight(after(part, ahead))
    ahead = exchange(ahead)

    kept = [(ROWS, 2048), (ROWS, 2048), (ROWS, MODEL), (ROWS, 128), (ROWS, 128), (8, 128, MODEL)]
    types = [BF16, BF16, BF16, BF16, F32, BF16]
    x_t, mixed, grad_t, bc_t, raw_t, other = call(
        temporal_forward_kernel,
        tuple(pltpu.HBM(dims, dtype) for dims, dtype in zip(kept, types)),
        [smem()] + vmem(2) + [smem()],
        [wide]
        + [pltpu.VMEM(dims, dtype) for dims, dtype in zip(kept, types)]
        + [pltpu.SemaphoreType.DMA((15,))],
        4,
        20,
        out_specs=hbm(6),
    )(core, ahead, decay_rate, gain)

    got = across("tm", other, 1)
    partial = call(
        weight_grad_kernel,
        (pltpu.HBM((8, 128, MODEL), BF16),),
        [smem()] + vmem(3),
        [pltpu.VMEM((8, 128, MODEL), BF16), pltpu.SemaphoreType.DMA((4,))],
        3,
        14,
        out_specs=hbm(1),
    )(core, mixed, grad_t, got)[0]
    grad_w = lax.psum_scatter(
        partial, "tm", scatter_dimension=0, axis_index_groups=along_z, tiled=False
    )
    raw_t = after(raw_t, partial)

    back = call(
        temporal_backward_kernel,
        shape(ROWS * SENT, 128),
        [smem()] + hbm(5) + [pl.BlockSpec(memory_space=pl.ANY)] * 2 + vmem(1) + [smem()],
        [wide, pltpu.VMEM((16, 2, 4, 16, MODEL), BF16), pltpu.VMEM((ROWS, 2048), BF16)]
        + [pltpu.VMEM(dims, dtype) for dims, dtype in zip(kept[:5], types)]
        + scan_scratch()
        + [pltpu.SemaphoreType.DMA((37,))],
        7,
        24,
    )(core, *in_hbm(x_t, mixed, grad_t, bc_t, raw_t), mine, theirs, decay_rate, gain)
    back = exchange(back)

    mixed_out, grad_x, grad_bc, grad_step = call(
        spatial_backward_kernel,
        (shape(ROWS, MODEL), shape(ROWS, 2048), shape(ROWS, 256), shape(2 * HEADS, ROWS)),
        vmem(5),
        [wide] + scan_scratch()[:2] + [pltpu.VMEM((ROWS, 2048), F32)],
        8,
        18,
    )(x, back, bc, raw, decay_rate)
    return (mixed_out[None], grad_x[None], grad_bc[None], grad_step.T[None], grad_w.astype(F32))


def solution(mesh):
    rows = P(("clip", "tm"), None, None)
    return jax.shard_map(
        on_device,
        mesh=mesh,
        in_specs=(rows, rows, rows, P(), P(), P("tm", None), rows),
        out_specs=(rows, rows, rows, rows, P(("clip", "tm"), None)),
        check_vma=False,
    )
```
